32 devices in a mesh: groups: 2 (over y), segment: 4 (over z), rows: 4 (over x, core).
Axes of the slice: x: 2, y: 2, z: 4, core: 2. Of those that a mesh axis runs over, the one named last changes fastest.
Arguments:
- hidden: bfloat16 [2, 32, 16, 320], P('groups', 'rows'), parts along dimension 0, may hold values from -36 to 36
- timesteps: int32 [2], P('groups'), parts along dimension 0, may hold values from 0 to 999
- rule_matrices: float32 [4, 4, 4, 4], P('segment'), may hold values from -2 to 2
- conv_factors: bfloat16 [4, 9, 4, 80, 80], P('segment'), may hold values from -0.0546875 to 0.0546875
- time_proj: bfloat16 [4, 320, 320], P('segment'), may hold values from -0.15625 to 0.15625
- skip_factors: bfloat16 [4, 4, 80, 80], P('segment'), may hold values from -0.15625 to 0.15625
- attn_factors: bfloat16 [4, 4, 4, 80, 80], P('segment'), may hold values from -0.3125 to 0.3125
- up_factors: bfloat16 [4, 4, 80, 320], P('segment'), may hold values from -0.3125 to 0.3125
- down_factors: bfloat16 [4, 4, 320, 80], P('segment'), may hold values from -0.15625 to 0.15625
- norm_gains: float32 [4, 3, 320], P('segment'), may hold values from 0.25 to 1.75
- head_scales: float32 [4, 5], P('segment'), may hold values from 3 to 12
- has_block: int32 [4], P('segment'), may hold values 0 or 1
- offsets: int32 [4], P('segment'), may hold values from 0 to 7
Outputs:
- states: bfloat16 [4, 2, 32, 16, 320], P('segment', 'groups', 'rows'), parts along dimension 1
The draws below stay inside these ranges and needn't reach their ends.
There are 2 independent parts, one for each index of `groups`. The reference program is written for one: setup_inputs(seed, part) draws one part's arguments, and reference() takes and returns one part's arrays. A program takes and returns all parts, laid end to end along the dimension named above; an argument that names none is the same for every part. Nothing has to cross between parts.
All inputs are finite; a program needn't handle non-finite values. No bound on the sum of `has_block` on one device may be relied on, other than what follows from the above.
Results may differ from the reference program's by a relative error of at most 0.0062.
Values may be sent and summed in bfloat16 or wider, within the bound.
No kernel may reach another device: no remote copies, remote signals or barrier semaphores. Data moves between devices by JAX's collectives and lax.ppermute only.
A program may use at most 64 MiB of HBM per device.

```python
import math
import jax
import jax.numpy as jnp
from jax import lax

C = 320
FF = 1280
HEADS = 5
HEAD = 64
QUAT = 4
WIN = 8
COLS = 16
NSTEPS = 1000
SECTIONS = 4
MB = 1
LROWS = 32


def draw_hidden(key, part):
    shape_all = (MB, LROWS, COLS, C)
    token_log = jax.random.uniform(jax.random.fold_in(key, 11), (MB, LROWS, COLS, 1), jnp.float32, -1.0, 1.0)
    channel_log = jax.random.uniform(jax.random.fold_in(key, 12), (1, 1, 1, C), jnp.float32, -1.0, 1.0)
    spread = 1.1513
    noise_part = jax.random.truncated_normal(jax.random.fold_in(key, 13), -3.0, 3.0, shape_all, jnp.float32)
    values = noise_part * jnp.exp(spread * token_log) * jnp.exp(spread * channel_log)
    return values.astype(jnp.bfloat16)


def touch_ends(array, own_key, least, high):
    place = [jax.random.randint(jax.random.fold_in(own_key, axis), (), 0, length) for axis, length in enumerate(array.shape)]
    longest = array.shape.index(max(array.shape))
    neighbour = place[:longest] + [(place[longest] + 1) % array.shape[longest]] + place[longest + 1:]
    return array.at[tuple(place)].set(least).at[tuple(neighbour)].set(high)


def block_scale(rng, shape, pieces, smallest, largest):
    def one(dim, shards_of):
        steps = jax.random.uniform(jax.random.fold_in(jax.random.fold_in(rng, 6), dim), (shards_of,), jnp.float32, smallest / len(pieces), largest / len(pieces))
        return jnp.repeat(jnp.exp(steps), shape[dim] // shards_of).reshape((-1,) + (1,) * (len(shape) - dim - 1))

    gain = one(*pieces[0])
    for cut in pieces[1:]:
        gain = gain * one(*cut)
    return gain


def noise(own_key, shape, deviation, reach, cuts=(), held_as=jnp.bfloat16):
    gain = block_scale(own_key, shape, cuts, -0.22, 0.18) if cuts else 1.0
    values = jax.random.normal(own_key, shape, jnp.float32) * deviation * gain
    return jnp.minimum(jnp.maximum(values, -reach), reach).astype(held_as)


def setup_inputs(seed: int = 0, part: int = 0) -> dict:
    key_list = jax.random.split(jax.random.key(seed), 14)
    part_keys = jax.random.split(jax.random.fold_in(key_list[13], part), 14)
    return {
        "hidden": draw_hidden(jax.random.fold_in(jax.random.fold_in(key_list[13], part), 71), part),
        "timesteps": jax.random.randint(part_keys[1], (MB,), 0, NSTEPS).astype(jnp.int32),
        "rule_matrices": noise(key_list[2], (SECTIONS, QUAT, QUAT, QUAT), 0.5, 2.0, ((0, 4),), jnp.float32),
        "conv_factors": noise(key_list[3], (SECTIONS, 9, QUAT, C // QUAT, C // QUAT), (36 * C) ** -0.5, 0.0546875, ((0, 4),)),
        "time_proj": noise(key_list[4], (SECTIONS, C, C), (4 * C) ** -0.5, 0.15625, ((0, 4),)),
        "skip_factors": noise(key_list[5], (SECTIONS, QUAT, C // QUAT, C // QUAT), (4 * C) ** -0.5, 0.15625, ((0, 4),)),
        "attn_factors": noise(key_list[6], (SECTIONS, 4, QUAT, C // QUAT, C // QUAT), C ** -0.5, 0.3125, ((0, 4),)),
        "up_factors": noise(key_list[7], (SECTIONS, QUAT, C // QUAT, FF // QUAT), C ** -0.5, 0.3125, ((0, 4),)),
        "down_factors": noise(key_list[8], (SECTIONS, QUAT, FF // QUAT, C // QUAT), FF ** -0.5, 0.15625, ((0, 4),)),
        "norm_gains": jnp.clip(1.0 + 0.15 * jax.random.normal(key_list[9], (SECTIONS, 3, C), jnp.float32), 0.25, 1.75),
        "head_scales": jnp.clip(jnp.exp(math.log(12.0) - 1.3862944 * jax.random.uniform(key_list[10], (SECTIONS, HEADS), jnp.float32) ** block_scale(key_list[10], (SECTIONS, HEADS), ((0, 4),), -0.2, 0.2)), 3.0, 12.0),
        "has_block": touch_ends((jax.random.randint(key_list[11], (SECTIONS,), 0, 2) < 1).astype(jnp.int32), jax.random.fold_in(key_list[11], 1), 0, 1),
        "offsets": touch_ends(jax.random.randint(key_list[12], (SECTIONS,), 0, WIN), jax.random.fold_in(key_list[12], 1), 0, WIN - 1).astype(jnp.int32),
    }


EPSILON = 1e-05
COS_EPSILON = 1e-06

def dense_weight(rule_mat, factors):
    expanded = jnp.einsum('iab,ipq->apbq', rule_mat.astype(jnp.float32), factors.astype(jnp.float32), precision=lax.Precision.HIGHEST)
    size_in = expanded.shape[0] * expanded.shape[1]
    size_out = expanded.shape[2] * expanded.shape[3]
    return expanded.reshape(size_in, size_out).astype(jnp.bfloat16)

def rms_scale(values, gain_row):
    mean_square = lax.optimization_barrier(jnp.mean(values * values, axis=-1, keepdims=True))
    return values * lax.rsqrt(mean_square + EPSILON) * gain_row

def time_features(timesteps):
    half_width = C // 2
    frequency = jnp.exp(-math.log(10000.0) * jnp.arange(half_width, dtype=jnp.float32) / half_width)
    angles = timesteps.astype(jnp.float32)[:, None] * frequency[None, :]
    return jnp.concatenate([jnp.cos(angles), jnp.sin(angles)], axis=-1).astype(jnp.bfloat16)

def conv_grid(normed, conv_taps):
    batch_count, height, columns, channels = normed.shape
    padded = jnp.pad(normed, ((0, 0), (1, 1), (1, 1), (0, 0))).astype(jnp.float32)
    pre_act = jnp.zeros((batch_count, height, columns, conv_taps.shape[-1]), jnp.float32)
    for tap_row in range(3):
        for tap_col in range(3):
            tap_slice = padded[:, tap_row:tap_row + height, tap_col:tap_col + columns, :]
            pre_act = pre_act + jnp.einsum('mrcx,xy->mrcy', tap_slice, conv_taps[3 * tap_row + tap_col].astype(jnp.float32))
    return pre_act

def window_attention(normed, qkv_dense, out_dense, scale_heads, offset_val):
    batch_count, height, columns, channels = normed.shape
    projected = jnp.einsum('mrcx,xy->mrcy', normed.astype(jnp.float32), qkv_dense.astype(jnp.float32)).astype(jnp.bfloat16)
    rolled = jnp.roll(projected, -offset_val, axis=2)
    grouped = rolled.reshape(batch_count, height // WIN, WIN, columns // WIN, WIN, 3, HEADS, HEAD)
    grouped = grouped.transpose(0, 1, 3, 2, 4, 5, 6, 7).reshape(batch_count, height // WIN, columns // WIN, WIN * WIN, 3, HEADS, HEAD)
    query_raw = grouped[:, :, :, :, 0].astype(jnp.float32)
    key_raw = grouped[:, :, :, :, 1].astype(jnp.float32)
    value_part = grouped[:, :, :, :, 2].astype(jnp.float32)
    query_unit = query_raw / jnp.sqrt(lax.optimization_barrier(jnp.sum(query_raw * query_raw, axis=-1, keepdims=True)) + COS_EPSILON)
    key_unit = key_raw / jnp.sqrt(lax.optimization_barrier(jnp.sum(key_raw * key_raw, axis=-1, keepdims=True)) + COS_EPSILON)
    scores = jnp.einsum('mijqhd,mijkhd->mijhqk', query_unit, key_unit, precision=lax.Precision.HIGHEST) * scale_heads[:, None, None]
    exp_scores = jnp.exp(scores)
    attention_probs = (exp_scores / lax.optimization_barrier(jnp.sum(exp_scores, axis=-1, keepdims=True))).astype(jnp.bfloat16)
    mixed_heads = jnp.einsum('mijhqk,mijkhd->mijqhd', attention_probs.astype(jnp.float32), value_part).astype(jnp.bfloat16)
    mixed_heads = mixed_heads.reshape(batch_count, height // WIN, columns // WIN, WIN, WIN, channels)
    mixed_heads = mixed_heads.transpose(0, 1, 3, 2, 4, 5).reshape(batch_count, height, columns, channels)
    mixed_heads = jnp.roll(mixed_heads, offset_val, axis=2)
    return jnp.einsum('mrcx,xy->mrcy', mixed_heads.astype(jnp.float32), out_dense.astype(jnp.float32))

def block_pass(after_conv, gain_rows, qkv_dense, out_dense, up_dense, down_dense, scale_heads, offset_val):
    normed = rms_scale(after_conv, gain_rows[1]).astype(jnp.bfloat16)
    attended = after_conv + window_attention(normed, qkv_dense, out_dense, scale_heads, offset_val)
    normed_mlp = rms_scale(attended, gain_rows[2]).astype(jnp.bfloat16)
    inner_act = jax.nn.silu(jnp.einsum('mrcx,xy->mrcy', normed_mlp.astype(jnp.float32), up_dense.astype(jnp.float32))).astype(jnp.bfloat16)
    return attended + jnp.einsum('mrcy,yx->mrcx', inner_act.astype(jnp.float32), down_dense.astype(jnp.float32))

def run_section(section, stream_in, skip_state, temb_all, rule_matrices, conv_factors, time_proj, skip_factors, attn_factors, up_factors, down_factors, norm_gains, head_scales, has_block, offsets):
    rule_mat = rule_matrices[section]
    conv_taps = jnp.stack([dense_weight(rule_mat, conv_factors[section, tap_index]) for tap_index in range(9)])
    qkv_dense = jnp.concatenate([dense_weight(rule_mat, attn_factors[section, part_index]) for part_index in range(3)], axis=1)
    out_dense = dense_weight(rule_mat, attn_factors[section, 3])
    up_dense = dense_weight(rule_mat, up_factors[section])
    down_dense = dense_weight(rule_mat, down_factors[section])
    gain_rows = norm_gains[section]
    stream = stream_in.astype(jnp.float32)
    normed = rms_scale(stream, gain_rows[0]).astype(jnp.bfloat16)
    pre_act = conv_grid(normed, conv_taps)
    time_term = jnp.dot(temb_all, time_proj[section], preferred_element_type=jnp.float32)
    pre_act = pre_act + time_term[:, None, None, :]
    if skip_state is not None:
        skip_dense = dense_weight(rule_mat, skip_factors[section])
        pre_act = pre_act + jnp.einsum('mrcx,xy->mrcy', skip_state.astype(jnp.float32), skip_dense.astype(jnp.float32))
    after_conv = stream + jax.nn.silu(pre_act)
    blocked = block_pass(after_conv, gain_rows, qkv_dense, out_dense, up_dense, down_dense, head_scales[section], offsets[section])
    result = jnp.where(has_block[section] == 1, blocked, after_conv)
    return result.astype(jnp.bfloat16)

def reference(hidden, timesteps, rule_matrices, conv_factors, time_proj, skip_factors, attn_factors, up_factors, down_factors, norm_gains, head_scales, has_block, offsets):
    half_count = SECTIONS // 2
    temb_all = time_features(timesteps)
    outputs = [None] * SECTIONS
    previous = hidden
    for section in range(SECTIONS):
        if section >= half_count:
            skip_state = outputs[section - half_count]
        else:
            skip_state = None
        result = run_section(section, previous, skip_state, temb_all, rule_matrices, conv_factors, time_proj, skip_factors, attn_factors, up_factors, down_factors, norm_gains, head_scales, has_block, offsets)
        outputs[section] = result
        previous = result
    return jnp.stack(outputs)
```

```python
import functools
import math

import jax
import jax.numpy as jnp
from jax import lax
from jax.experimental import pallas as pl
from jax.experimental.pallas import tpu as pltpu
from jax.sharding import PartitionSpec as P

HEADS = 5
HEAD = 64
WIN = 8
QUAT = 4

EPSILON = 1e-05
COS_EPSILON = 1e-06

F32 = jnp.float32
BF16 = jnp.bfloat16
MIB = 1024 * 1024

VMEM = pl.BlockSpec(memory_space=pltpu.VMEM)
SMEM = pl.BlockSpec(memory_space=pltpu.SMEM)


def in_vmem(value):
    return pltpu.with_memory_space_constraint(value, pltpu.VMEM)


def dot(left, right):
    return jnp.dot(left, right, preferred_element_type=F32)


def rms(values, gain_row):
    mean_square = jnp.mean(values * values, axis=-1, keepdims=True)
    return values * lax.rsqrt(mean_square + EPSILON) * gain_row


def silu(values):
    return values / (1.0 + jnp.exp(-values))


def weights_kernel(
    rule_ref, time_ref, conv_ref, skip_ref, attn_ref, up_ref, down_ref, proj_ref,
    mix_out, attn_out, up_out, down_out, term_out,
):
    part = conv_ref.shape[-1]

    def rule(i, a, b):
        return rule_ref[(i * QUAT + a) * QUAT + b]

    def block_row(factors, a):
        blocks = []
        for b in range(QUAT):
            total = factors[0] * rule(0, a, b)
            for i in range(1, QUAT):
                total = total + factors[i] * rule(i, a, b)
            blocks.append(total)
        return blocks

    def square(load, store):
        factors = [load(i).astype(F32) for i in range(QUAT)]
        for a in range(QUAT):
            store(a, jnp.concatenate(block_row(factors, a), axis=1).astype(BF16))

    def conv_step(tap, carry):
        def store(a, value):
            mix_out[tap, a * part : (a + 1) * part, :] = value

        square(lambda i: conv_ref[tap, i], store)
        return carry

    lax.fori_loop(0, 9, conv_step, 0)

    def skip_store(a, value):
        mix_out[9, a * part : (a + 1) * part, :] = value

    square(lambda i: skip_ref[i], skip_store)

    def attn_step(which, carry):
        def store(a, value):
            attn_out[which, a * part : (a + 1) * part, :] = value

        square(lambda i: attn_ref[which, i], store)
        return carry

    lax.fori_loop(0, 4, attn_step, 0)

    wide = down_ref.shape[1]
    for chunk in range(wide // part):
        def store(a, value):
            down_out[a * wide + chunk * part : a * wide + (chunk + 1) * part, :] = value

        square(lambda i: down_ref[i, chunk * part : (chunk + 1) * part, :], store)

    for chunk in range(part // 16):
        rows = slice(chunk * 16, (chunk + 1) * 16)
        factors = [up_ref[i, rows, :].astype(F32) for i in range(QUAT)]
        for a in range(QUAT):
            for b, value in enumerate(block_row(factors, a)):
                start = a * part + chunk * 16
                up_out[b, start : start + 16, :] = value.astype(BF16)

    channels = proj_ref.shape[0]
    half = channels // 2
    lane = lax.broadcasted_iota(jnp.int32, (8, channels), 1)
    place = jnp.where(lane < half, lane, lane - half).astype(F32)
    frequency = jnp.exp(-math.log(10000.0) * place / half)
    for batch in range(term_out.shape[0]):
        angles = time_ref[batch].astype(F32) * frequency
        features = jnp.where(lane < half, jnp.cos(angles), jnp.sin(angles)).astype(BF16)
        term_out[batch] = dot(features, proj_ref[...])


def section_weights(rule, timesteps, conv, skip, attn, up, down, proj):
    channels = proj.shape[0]
    return pl.pallas_call(
        weights_kernel,
        out_shape=(
            pltpu.VMEM((10, channels, channels), BF16),
            pltpu.VMEM((4, channels, channels), BF16),
            pltpu.VMEM((QUAT, channels, up.shape[-1]), BF16),
            pltpu.VMEM((QUAT * down.shape[1], channels), BF16),
            pltpu.VMEM((timesteps.shape[0], 8, channels), F32),
        ),
        in_specs=[SMEM, SMEM] + [VMEM] * 6,
        out_specs=(VMEM,) * 5,
        compiler_params=pltpu.CompilerParams(vmem_limit_bytes=24 * MIB),
        name="weights",
    )(rule.reshape(-1), timesteps, conv, skip, attn, up, down, proj)


def section_kernel(
    columns, with_skip, flags_ref, scales_ref, x_ref, low_ref, high_ref, *rest,
):
    if with_skip:
        z_ref, prev_ref, mix_ref, attn_ref, up_ref, down_ref, term_ref, gain_ref, out_ref = rest
    else:
        prev_ref, mix_ref, attn_ref, up_ref, down_ref, term_ref, gain_ref, out_ref = rest
    active, has_block, offset = flags_ref[0], flags_ref[1], flags_ref[2]
    tokens, channels = x_ref.shape

    @pl.when(active == 0)
    def _():
        out_ref[...] = prev_ref[...]

    @pl.when(active == 1)
    def _():
        gain = [gain_ref[row : row + 1, :] for row in range(3)]
        main = x_ref[...].astype(F32)
        ext = jnp.concatenate(
            [low_ref[...].astype(F32), main, high_ref[...].astype(F32)], axis=0
        )
        total = ext.shape[0]
        normed = rms(ext, gain[0])
        col = lax.rem(lax.broadcasted_iota(jnp.int32, (total, 1), 0), columns)
        left = jnp.where(col == 0, 0.0, pltpu.roll(normed, 1, 0)).astype(BF16)
        right = jnp.where(col == columns - 1, 0.0, pltpu.roll(normed, total - 1, 0)).astype(BF16)
        shifted = [left, normed.astype(BF16), right]
        hidden = jnp.broadcast_to(term_ref[0:1, :], (tokens, channels))
        if with_skip:
            hidden = hidden + dot(z_ref[...], mix_ref[9])
        for a in range(3):
            for b in range(3):
                rows = shifted[b][a * columns : a * columns + tokens]
                hidden = hidden + dot(rows, mix_ref[3 * a + b])
        x1 = main + silu(hidden)

        @pl.when(has_block == 0)
        def _():
            out_ref[...] = x1.astype(BF16)

        @pl.when(has_block == 1)
        def _():
            n2 = rms(x1, gain[1]).astype(BF16)
            query = dot(n2, attn_ref[0]).astype(BF16)
            keys = dot(n2, attn_ref[1]).astype(BF16)
            value = dot(n2, attn_ref[2]).astype(BF16)

            def window(index):
                c = lax.rem(index, columns)
                return lax.rem(c - offset + columns, columns) // WIN

            row_w = window(lax.broadcasted_iota(jnp.int32, (tokens, tokens), 0))
            col_w = window(lax.broadcasted_iota(jnp.int32, (tokens, tokens), 1))
            same = row_w == col_w
            mixed = []
            for head in range(HEADS):
                lanes = slice(head * HEAD, (head + 1) * HEAD)
                q, k, v = query[:, lanes], keys[:, lanes], value[:, lanes]
                qf, kf = q.astype(F32), k.astype(F32)
                q_scale = lax.rsqrt(jnp.sum(qf * qf, axis=-1, keepdims=True) + COS_EPSILON)
                k_scale = lax.rsqrt(jnp.sum(kf * kf, axis=-1, keepdims=True) + COS_EPSILON)
                raw = lax.dot_general(
                    q, k, (((1,), (1,)), ((), ())), preferred_element_type=F32
                )
                scores = raw * (q_scale * scales_ref[head]) * jnp.transpose(k_scale)
                weight = jnp.where(same, jnp.exp(scores), 0.0)
                prob = (weight / jnp.sum(weight, axis=-1, keepdims=True)).astype(BF16)
                mixed.append(dot(prob, v))
            heads = jnp.concatenate(mixed, axis=1).astype(BF16)
            x2 = x1 + dot(heads, attn_ref[3])
            n3 = rms(x2, gain[2]).astype(BF16)
            wide = up_ref.shape[-1]
            x3 = x2
            for b in range(QUAT):
                act = silu(dot(n3, up_ref[b])).astype(BF16)
                x3 = x3 + dot(act, down_ref[b * wide : (b + 1) * wide, :])
            out_ref[...] = x3.astype(BF16)


def run_section(columns, flags, scales, x, low, high, z, prev, weights, term, gains):
    mix, attn, up, down = weights
    with_skip = z is not None
    operands = [flags, scales, x, low, high] + ([z] if with_skip else []) + [prev]
    operands += [in_vmem(w) for w in (mix, attn, up, down)] + [term, gains]
    return pl.pallas_call(
        functools.partial(section_kernel, columns, with_skip),
        out_shape=jax.ShapeDtypeStruct(x.shape, BF16),
        in_specs=[SMEM, SMEM] + [VMEM] * (len(operands) - 2),
        out_specs=VMEM,
        compiler_params=pltpu.CompilerParams(vmem_limit_bytes=24 * MIB),
        name="section",
    )(*operands)


def shards(
    hidden, timesteps, rule_matrices, conv_factors, time_proj, skip_factors, attn_factors,
    up_factors, down_factors, norm_gains, head_scales, has_block, offsets,
):
    segments = lax.axis_size("segment")
    row_parts = lax.axis_size("rows")
    half = segments // 2
    segment = lax.axis_index("segment")
    batches, height, columns, channels = hidden.shape
    tokens = height * columns
    axes = ("segment", "rows")

    def pairs(sources, step, turn):
        return [
            (s * row_parts + r, (s + step) * row_parts + r + turn)
            for s in sources
            for r in range(row_parts)
            if s + step < segments and 0 <= r + turn < row_parts
        ]

    def pass_on(value, sources, step, turn):
        links = pairs(sources, step, turn)
        if not links:
            return jnp.zeros_like(value)
        return lax.ppermute(value, axes, links)

    flat = hidden.reshape(batches, tokens, channels)
    low0 = pass_on(flat[:, tokens - columns :], [0], 0, 1)
    high0 = pass_on(flat[:, :columns], [0], 0, -1)
    *weights, terms = section_weights(
        rule_matrices[0], timesteps, conv_factors[0], skip_factors[0], attn_factors[0],
        up_factors[0], down_factors[0], time_proj[0],
    )

    def section(active, x, low, high, z, prev, term):
        flags = jnp.stack([active.astype(jnp.int32), has_block[0], offsets[0]])
        return run_section(
            columns, flags, head_scales[0], x, low, high, z, prev, weights, term, norm_gains[0]
        )

    def edges_on(out, sources):
        main = pass_on(out, sources, 1, 0)
        low = pass_on(out[tokens - columns :], sources, 1, 1)
        high = pass_on(out[:columns], sources, 1, -1)
        return main, low, high

    if batches == 1:
        x, low, high = flat[0], low0[0], high0[0]
        out = flat[0]
        skips = []
        for tick in range(segments):
            z = skips[tick - half] if tick >= half else None
            out = section(segment == tick, x, low, high, z, out, terms[0])
            if tick + 1 < segments:
                x, low, high = edges_on(out, [tick])
                skips.append(pass_on(out, [tick], half, 0) if tick + half < segments else None)
        return out.reshape(1, batches, height, columns, channels)

    def pick(array, slot):
        return lax.dynamic_index_in_dim(array, slot, 0, keepdims=False)

    def tick_step(tick, state):
        states, received, skip_buffer = state
        batch = tick - segment
        active = (batch >= 0) & (batch < batches)
        slot = jnp.clip(batch, 0, batches - 1)
        first = [pick(array, slot) for array in (flat, low0, high0)]
        x, low, high = [jnp.where(segment == 0, f, r) for f, r in zip(first, received)]
        out = section(
            active, x, low, high, pick(skip_buffer, slot), pick(states, slot), pick(terms, slot)
        )
        states = lax.dynamic_update_index_in_dim(states, out, slot, 0)
        passed = edges_on(out, range(segments))
        arrived = pass_on(out, range(segments), half, 0)
        partner = tick - segment + half
        fits = (segment >= half) & (partner >= 0) & (partner < batches)
        partner_slot = jnp.clip(partner, 0, batches - 1)
        kept = pick(skip_buffer, partner_slot)
        skip_buffer = lax.dynamic_update_index_in_dim(
            skip_buffer, jnp.where(fits, arrived, kept), partner_slot, 0
        )
        return states, passed, skip_buffer

    edge = jnp.zeros((columns, channels), BF16)
    initial = (jnp.zeros_like(flat), (jnp.zeros_like(flat[0]), edge, edge), jnp.zeros_like(flat))
    states = lax.fori_loop(0, batches + segments - 1, tick_step, initial)[0]
    return states.reshape(1, batches, height, columns, channels)


def solution(mesh):
    return jax.shard_map(
        shards,
        mesh=mesh,
        in_specs=(
            P("groups", "rows", None, None),
            P("groups"),
            P("segment", None, None, None),
            P("segment", None, None, None, None),
            P("segment", None, None),
            P("segment", None, None, None),
            P("segment", None, None, None, None),
            P("segment", None, None, None),
            P("segment", None, None, None),
            P("segment", None, None),
            P("segment", None),
            P("segment"),
            P("segment"),
        ),
        out_specs=P("segment", "groups", "rows", None, None),
        check_vma=False,
    )
```

```python
import functools
import math

import jax
import jax.numpy as jnp
from jax import lax
from jax.experimental import pallas as pl
from jax.experimental.pallas import tpu as pltpu
from jax.sharding import PartitionSpec as P

HEADS = 5
HEAD = 64
WIN = 8
QUAT = 4

EPSILON = 1e-05
COS_EPSILON = 1e-06

F32 = jnp.float32
BF16 = jnp.bfloat16
MIB = 1024 * 1024

VMEM = pl.BlockSpec(memory_space=pltpu.VMEM)
SMEM = pl.BlockSpec(memory_space=pltpu.SMEM)
HBM = pl.BlockSpec(memory_space=pltpu.HBM)


def in_vmem(value):
    return pltpu.with_memory_space_constraint(value, pltpu.VMEM)


def in_smem(value):
    return pltpu.with_memory_space_constraint(value, pltpu.SMEM)


def in_hbm(value):
    return pltpu.with_memory_space_constraint(value, pltpu.HBM)


def dot(left, right):
    return jnp.dot(left, right, preferred_element_type=F32)


def dot_t(left, right):
    return lax.dot_general(left, right, (((1,), (1,)), ((), ())), preferred_element_type=F32)


def rms(values, gain_row):
    mean_square = jnp.mean(values * values, axis=-1, keepdims=True)
    return values * lax.rsqrt(mean_square + EPSILON) * gain_row


def silu(values):
    return values / (1.0 + jnp.exp(-values))


def weights_kernel(
    rule_hbm, time_hbm, flag_hbm, offset_hbm, scale_hbm, gain_hbm,
    conv_hbm, attn_hbm, up_hbm, down_hbm, skip_hbm, proj_hbm,
    mix_out, attn_out, up_out, down_out, term_out, gain_out, meta_out, scale_out,
    rule_ref, time_ref, flag_ref, offset_ref, conv_ref, attn_ref, up_ref, down_ref,
    skip_ref, proj_ref, sems,
):
    sources = [
        rule_hbm, conv_hbm, skip_hbm, time_hbm, proj_hbm, flag_hbm, offset_hbm, scale_hbm,
        gain_hbm, attn_hbm, up_hbm, down_hbm,
    ]
    targets = [
        rule_ref, conv_ref, skip_ref, time_ref, proj_ref, flag_ref, offset_ref, scale_out,
        gain_out, attn_ref, up_ref, down_ref,
    ]
    copies = [
        pltpu.make_async_copy(source, target, sems.at[place])
        for place, (source, target) in enumerate(zip(sources, targets))
    ]
    for copy in copies:
        copy.start()
    part = conv_ref.shape[-1]

    def rule(i, a, b):
        return rule_ref[i, a, b]

    def block_row(factors, a):
        blocks = []
        for b in range(QUAT):
            total = factors[0] * rule(0, a, b)
            for i in range(1, QUAT):
                total = total + factors[i] * rule(i, a, b)
            blocks.append(total)
        return blocks

    def square(load, store):
        factors = [load(i).astype(F32) for i in range(QUAT)]
        for a in range(QUAT):
            store(a, jnp.concatenate(block_row(factors, a), axis=1).astype(BF16))

    copies[0].wait()
    copies[1].wait()

    def conv_step(tap, carry):
        def store(a, value):
            mix_out[tap, a * part : (a + 1) * part, :] = value

        square(lambda i: conv_ref[tap, i], store)
        return carry

    lax.fori_loop(0, 9, conv_step, 0)

    copies[2].wait()

    def skip_store(a, value):
        mix_out[9, a * part : (a + 1) * part, :] = value

    square(lambda i: skip_ref[i], skip_store)

    for copy in copies[3:9]:
        copy.wait()
    channels = proj_ref.shape[0]
    half = channels // 2
    lane = lax.broadcasted_iota(jnp.int32, (8, channels), 1)
    place = jnp.where(lane < half, lane, lane - half).astype(F32)
    frequency = jnp.exp(-math.log(10000.0) * place / half)
    for batch in range(term_out.shape[0]):
        angles = time_ref[batch].astype(F32) * frequency
        features = jnp.where(lane < half, jnp.cos(angles), jnp.sin(angles)).astype(BF16)
        term_out[batch] = dot(features, proj_ref[...])
    meta_out[0] = flag_ref[0]
    meta_out[1] = offset_ref[0]
    for copy in copies[9:]:
        copy.wait()

    @pl.when(flag_ref[0] == 1)
    def _():
        def attn_step(which, carry):
            def store(a, value):
                attn_out[which, a * part : (a + 1) * part, :] = value

            square(lambda i: attn_ref[which, i], store)
            return carry

        lax.fori_loop(0, 4, attn_step, 0)

        def wide_step(chunk, carry):
            start = pl.multiple_of(chunk * 16, 16)
            ups = [up_ref[i, pl.ds(start, 16), :].astype(F32) for i in range(QUAT)]
            downs = [down_ref[i, pl.ds(start, 16), :].astype(F32) for i in range(QUAT)]
            for a in range(QUAT):
                rows = pl.ds(pl.multiple_of(a * part + start, 16), 16)
                for b, value in enumerate(block_row(ups, a)):
                    up_out[b, rows, :] = value.astype(BF16)
            for b in range(QUAT):
                rows = pl.ds(pl.multiple_of(b * part + start, 16), 16)
                for a in range(QUAT):
                    total = downs[0] * rule(0, a, b)
                    for i in range(1, QUAT):
                        total = total + downs[i] * rule(i, a, b)
                    down_out[a, rows, :] = total.astype(BF16)
            return carry

        lax.fori_loop(0, part // 16, wide_step, 0)


def section_weights(rule, timesteps, flag, offset, scales, gains, conv, attn, up, down, skip, proj):
    channels = proj.shape[0]
    wide = up.shape[-1]
    operands = (rule, timesteps, flag, offset, scales, gains, conv, attn, up, down, skip, proj)
    return pl.pallas_call(
        weights_kernel,
        out_shape=(
            pltpu.VMEM((10, channels, channels), BF16),
            pltpu.VMEM((4, channels, channels), BF16),
            pltpu.VMEM((QUAT, channels, wide), BF16),
            pltpu.VMEM((QUAT, channels, wide), BF16),
            pltpu.VMEM((timesteps.shape[0], 8, channels), F32),
            pltpu.VMEM(gains.shape, F32),
            pltpu.SMEM((2,), jnp.int32),
            pltpu.SMEM(scales.shape, F32),
        ),
        in_specs=[HBM] * len(operands),
        out_specs=(VMEM,) * 6 + (SMEM,) * 2,
        scratch_shapes=[
            pltpu.SMEM(rule.shape, F32),
            pltpu.SMEM(timesteps.shape, jnp.int32),
            pltpu.SMEM((1,), jnp.int32),
            pltpu.SMEM((1,), jnp.int32),
        ]
        + [pltpu.VMEM(array.shape, BF16) for array in (conv, attn, up, down, skip, proj)]
        + [pltpu.SemaphoreType.DMA((12,))],
        compiler_params=pltpu.CompilerParams(vmem_limit_bytes=10 * MIB),
        name="weights",
    )(*[in_hbm(v) if v.size > 1 else v for v in operands])


def is_active(tick, batches):
    batch = tick - lax.axis_index("segment")
    return (batch >= 0) & (batch < batches)


def shift_columns(normed, columns):
    total = normed.shape[0]
    col = lax.rem(lax.broadcasted_iota(jnp.int32, (total, 1), 0), columns)
    left = jnp.where(col == 0, 0.0, pltpu.roll(normed, 1, 0)).astype(BF16)
    right = jnp.where(col == columns - 1, 0.0, pltpu.roll(normed, total - 1, 0)).astype(BF16)
    return [left, normed.astype(BF16), right]


def inner_kernel(columns, tick, batches, with_skip, *refs):
    if tick is None:
        tick_ref, *refs = refs
        tick = tick_ref[0]
    if with_skip:
        z_ref, *refs = refs
    x_ref, mix_ref, term_ref, gain_ref, sum_ref = refs
    tokens, channels = x_ref.shape

    @pl.when(is_active(tick, batches))
    def _():
        shifted = shift_columns(rms(x_ref[...].astype(F32), gain_ref[0]), columns)
        edge = jnp.zeros((columns, channels), BF16)
        hidden = jnp.broadcast_to(term_ref[0:1, :], (tokens, channels))
        if with_skip:
            hidden = hidden + dot(z_ref[...], mix_ref[9])
        for b in range(3):
            hidden = hidden + dot(shifted[b], mix_ref[3 + b])
        for b in range(3):
            rows = jnp.concatenate([edge, shifted[b][: tokens - columns]], axis=0)
            hidden = hidden + dot(rows, mix_ref[b])
        for b in range(3):
            rows = jnp.concatenate([shifted[b][columns:], edge], axis=0)
            hidden = hidden + dot(rows, mix_ref[6 + b])
        sum_ref[...] = hidden


def outer_kernel(columns, tick, batches, *refs):
    if tick is None:
        tick_ref, *refs = refs
        tick = tick_ref[0]
    (
        meta_ref, scales_ref, x_ref, sum_ref, low_ref, high_ref, prev_ref, mix_ref, attn_ref,
        up_ref, down_ref, gain_ref, out_ref, first_ref, last_ref,
    ) = refs
    tokens, channels = x_ref.shape
    active = is_active(tick, batches)

    def write(x3):
        value = x3.astype(BF16)
        out_ref[...] = value
        first_ref[...] = value[:columns]
        last_ref[...] = value[tokens - columns :]

    @pl.when(jnp.logical_not(active))
    def _():
        out_ref[...] = prev_ref[...]

    @pl.when(active)
    def _():
        gain = [gain_ref[row] for row in range(3)]
        below = low_ref.shape[0] - columns
        low = shift_columns(rms(low_ref[below:].astype(F32), gain[0]), columns)
        high = shift_columns(rms(high_ref[:columns].astype(F32), gain[0]), columns)
        top = sum_ref[:columns]
        bottom = sum_ref[tokens - columns :]
        for b in range(3):
            top = top + dot(low[b], mix_ref[b])
            bottom = bottom + dot(high[b], mix_ref[6 + b])
        hidden = jnp.concatenate([top, sum_ref[columns : tokens - columns], bottom], axis=0)
        x1 = x_ref[...].astype(F32) + silu(hidden)
        has_block, offset = meta_ref[0], meta_ref[1]

        @pl.when(has_block != 1)
        def _():
            write(x1)

        @pl.when(has_block == 1)
        def _():
            n2 = rms(x1, gain[1]).astype(BF16)
            query = dot(n2, attn_ref[0]).astype(BF16)
            keys = dot(n2, attn_ref[1]).astype(BF16)
            value = dot(n2, attn_ref[2]).astype(BF16)

            def window(index):
                c = lax.rem(index, columns)
                return lax.rem(c - offset + columns, columns) // WIN

            row_w = window(lax.broadcasted_iota(jnp.int32, (tokens, tokens), 0))
            col_w = window(lax.broadcasted_iota(jnp.int32, (tokens, tokens), 1))
            same = row_w == col_w
            mixed = []
            for head in range(HEADS):
                lanes = slice(head * HEAD, (head + 1) * HEAD)
                q, k, v = query[:, lanes], keys[:, lanes], value[:, lanes]
                qf, kf = q.astype(F32), k.astype(F32)
                q_scale = lax.rsqrt(jnp.sum(qf * qf, axis=-1, keepdims=True) + COS_EPSILON)
                k_scale = lax.rsqrt(jnp.sum(kf * kf, axis=-1, keepdims=True) + COS_EPSILON)
                raw = dot_t(q, k)
                scores = raw * (q_scale * scales_ref[0, head]) * jnp.transpose(k_scale)
                weight = jnp.where(same, jnp.exp(scores), 0.0)
                prob = (weight / jnp.sum(weight, axis=-1, keepdims=True)).astype(BF16)
                mixed.append(dot(prob, v))
            heads = jnp.concatenate(mixed, axis=1).astype(BF16)
            x2 = x1 + dot(heads, attn_ref[3])
            n3 = rms(x2, gain[2]).astype(BF16)
            x3 = x2
            for b in range(QUAT):
                act = silu(dot(n3, up_ref[b])).astype(BF16)
                x3 = x3 + dot_t(act, down_ref[b])
            write(x3)


def run_inner(columns, tick, batches, x, z, mix, term, gains):
    static = isinstance(tick, int)
    with_skip = z is not None
    operands = [z] if with_skip else []
    operands += [x, in_vmem(mix), term, in_vmem(gains)]
    specs = [VMEM] * len(operands)
    if not static:
        operands, specs = [tick] + operands, [SMEM] + specs
    return pl.pallas_call(
        functools.partial(inner_kernel, columns, tick if static else None, batches, with_skip),
        out_shape=pltpu.VMEM(x.shape, F32),
        in_specs=specs,
        out_specs=VMEM,
        compiler_params=pltpu.CompilerParams(vmem_limit_bytes=8 * MIB),
        name="inner",
    )(*operands)


def run_outer(columns, tick, batches, x, total, low, high, prev, weights):
    static = isinstance(tick, int)
    mix, attn, up, down, gains, meta, scales = weights
    operands = [in_smem(meta), in_smem(scales), x, in_vmem(total), low, high, prev]
    operands += [in_vmem(w) for w in (mix, attn, up, down, gains)]
    specs = [SMEM] * 2 + [VMEM] * (len(operands) - 2)
    if not static:
        operands, specs = [tick] + operands, [SMEM] + specs
    edge = jax.ShapeDtypeStruct((columns, x.shape[1]), BF16)
    return pl.pallas_call(
        functools.partial(outer_kernel, columns, tick if static else None, batches),
        out_shape=(jax.ShapeDtypeStruct(x.shape, BF16), edge, edge),
        in_specs=specs,
        out_specs=(VMEM,) * 3,
        compiler_params=pltpu.CompilerParams(vmem_limit_bytes=8 * MIB),
        name="outer",
    )(*operands)


def shards(
    hidden, timesteps, rule_matrices, conv_factors, time_proj, skip_factors, attn_factors,
    up_factors, down_factors, norm_gains, head_scales, has_block, offsets,
):
    segments = lax.axis_size("segment")
    row_parts = lax.axis_size("rows")
    half = segments // 2
    segment = lax.axis_index("segment")
    batches, height, columns, channels = hidden.shape
    tokens = height * columns
    axes = ("segment", "rows")

    def pairs(sources, step, turn):
        return [
            (s * row_parts + r, (s + step) * row_parts + r + turn)
            for s in sources
            for r in range(row_parts)
            if s + step < segments and 0 <= r + turn < row_parts
        ]

    def pass_on(value, sources, step, turn):
        links = pairs(sources, step, turn)
        if not links:
            return jnp.zeros_like(value)
        return lax.ppermute(value, axes, links)

    flat = hidden.reshape(batches, tokens, channels)
    low0 = pass_on(flat, [0], 0, 1)
    high0 = pass_on(flat, [0], 0, -1)
    mix, attn, up, down, terms, gains, meta, scales = section_weights(
        rule_matrices[0], timesteps, has_block, offsets, head_scales,
        jnp.transpose(norm_gains, (1, 0, 2)), conv_factors[0], attn_factors[0], up_factors[0],
        jnp.transpose(down_factors[0], (0, 2, 1)), skip_factors[0], time_proj[0],
    )
    weights = (mix, attn, up, down, gains, meta, scales)

    def section(tick, x, low, high, z, prev, term):
        total = run_inner(columns, tick, batches, x, z, mix, term, gains)
        return run_outer(columns, tick, batches, x, total, low, high, prev, weights)

    def edges_on(out, first, last, sources):
        main = pass_on(out, sources, 1, 0)
        low = pass_on(last, sources, 1, 1)
        high = pass_on(first, sources, 1, -1)
        return main, low, high

    if batches == 1:
        x, low, high = flat[0], low0[0], high0[0]
        out = flat[0]
        skips = []
        for tick in range(segments):
            z = skips[tick - half] if tick >= half else None
            out, first, last = section(tick, x, low, high, z, out, terms[0])
            if tick + 1 < segments:
                x, low, high = edges_on(out, first, last, [tick])
                skips.append(pass_on(out, [tick], half, 0) if tick + half < segments else None)
        return out.reshape(1, batches, height, columns, channels)

    def pick(array, slot):
        return lax.dynamic_index_in_dim(array, slot, 0, keepdims=False)

    def tick_step(tick, state):
        states, received, skip_buffer = state
        slot = jnp.clip(tick - segment, 0, batches - 1)
        own = pick(flat, slot), pick(low0, slot)[tokens - columns :], pick(high0, slot)[:columns]
        x, low, high = [jnp.where(segment == 0, f, r) for f, r in zip(own, received)]
        out, first, last = section(
            jnp.reshape(tick, (1,)), x, low, high, pick(skip_buffer, slot), pick(states, slot),
            pick(terms, slot),
        )
        states = lax.dynamic_update_index_in_dim(states, out, slot, 0)
        passed = edges_on(out, first, last, range(segments))
        arrived = pass_on(out, range(segments), half, 0)
        partner = tick - segment + half
        fits = (segment >= half) & (partner >= 0) & (partner < batches)
        partner_slot = jnp.clip(partner, 0, batches - 1)
        kept = pick(skip_buffer, partner_slot)
        skip_buffer = lax.dynamic_update_index_in_dim(
            skip_buffer, jnp.where(fits, arrived, kept), partner_slot, 0
        )
        return states, passed, skip_buffer

    edge = jnp.zeros((columns, channels), BF16)
    initial = (jnp.zeros_like(flat), (jnp.zeros_like(flat[0]), edge, edge), jnp.zeros_like(flat))
    states = lax.fori_loop(0, batches + segments - 1, tick_step, initial)[0]
    return states.reshape(1, batches, height, columns, channels)


def solution(mesh):
    return jax.shard_map(
        shards,
        mesh=mesh,
        in_specs=(
            P("groups", "rows", None, None),
            P("groups"),
            P("segment", None, None, None),
            P("segment", None, None, None, None),
            P("segment", None, None),
            P("segment", None, None, None),
            P("segment", None, None, None, None),
            P("segment", None, None, None),
            P("segment", None, None, None),
            P("segment", None, None),
            P("segment", None),
            P("segment"),
            P("segment"),
        ),
        out_specs=P("segment", "groups", "rows", None, None),
        check_vma=False,
    )
```

```python
import functools
import math

import jax
import jax.numpy as jnp
from jax import lax
from jax.experimental import pallas as pl
from jax.experimental.pallas import tpu as pltpu
from jax.sharding import PartitionSpec as P

HEAD = 64
WIN = 8
QUAT = 4

EPSILON = 1e-05
COS_EPSILON = 1e-06

F32 = jnp.float32
BF16 = jnp.bfloat16
MIB = 1024 * 1024
LANES = 128

VMEM = pl.BlockSpec(memory_space=pltpu.VMEM)
SMEM = pl.BlockSpec(memory_space=pltpu.SMEM)
HBM = pl.BlockSpec(memory_space=pltpu.HBM)


def in_vmem(value):
    return pltpu.with_memory_space_constraint(value, pltpu.VMEM)


def in_smem(value):
    return pltpu.with_memory_space_constraint(value, pltpu.SMEM)


def in_hbm(value):
    return pltpu.with_memory_space_constraint(value, pltpu.HBM)


def dot(left, right):
    return jnp.dot(left, right, preferred_element_type=F32)


def dot_t(left, right):
    return lax.dot_general(left, right, (((1,), (1,)), ((), ())), preferred_element_type=F32)


def rms(values, gain_row):
    mean_square = jnp.mean(values * values, axis=-1, keepdims=True)
    return values * lax.rsqrt(mean_square + EPSILON) * gain_row


def silu(values):
    return values / (1.0 + jnp.exp(-values))


def weights_kernel(
    rule_hbm, time_hbm, flag_hbm, offset_hbm, scale_hbm, gain_hbm,
    conv_hbm, attn_hbm, up_hbm, down_hbm, skip_hbm, proj_hbm, hidden_hbm,
    mix_out, qkv_out, out_out, up_out, down_out, term_out, gain_out, meta_out, scale_out,
    hidden_out,
    rule_ref, time_ref, flag_ref, offset_ref, conv_ref, attn_ref, up_ref, down_ref,
    skip_ref, proj_ref, rows_ref, spread_ref, sems,
):
    sources = [
        rule_hbm, conv_hbm, skip_hbm, time_hbm, proj_hbm, flag_hbm, offset_hbm, scale_hbm,
        gain_hbm, hidden_hbm, attn_hbm, up_hbm, down_hbm,
    ]
    targets = [
        rule_ref, conv_ref, skip_ref, time_ref, proj_ref, flag_ref, offset_ref, scale_out,
        gain_out, hidden_out, attn_ref, up_ref, down_ref,
    ]
    copies = [
        pltpu.make_async_copy(source, target, sems.at[place])
        for place, (source, target) in enumerate(zip(sources, targets))
    ]
    for copy in copies:
        copy.start()
    part = conv_ref.shape[-1]

    def rule(i, a, b):
        return rule_ref[i, a, b]

    def block_row(factors, a):
        blocks = []
        for b in range(QUAT):
            total = factors[0] * rule(0, a, b)
            for i in range(1, QUAT):
                total = total + factors[i] * rule(i, a, b)
            blocks.append(total)
        return blocks

    channels = proj_ref.shape[0]
    tail = channels % LANES
    full = channels - tail
    padded = full + LANES

    def channel_of(lane):
        return jnp.where(lane < channels, lane, lane - tail)

    lanes = channel_of(lax.broadcasted_iota(jnp.int32, (part, padded), 1))
    ones = lax.rem(lanes, part) == lax.broadcasted_iota(jnp.int32, (part, padded), 0)
    repeat = jnp.where(ones, 1.0, 0.0).astype(BF16)
    copies[0].wait()
    block = channel_of(lax.broadcasted_iota(jnp.int32, (8, padded), 1)) // part
    for i in range(QUAT):
        for a in range(QUAT):
            row = jnp.where(block == 0, rule(i, a, 0), rule(i, a, 1))
            row = jnp.where(block == 2, rule(i, a, 2), row)
            rows_ref[i * QUAT + a] = jnp.where(block == 3, rule(i, a, 3), row)

    def square(slot, factors, store):
        spread_ref[slot] = dot(factors.reshape(QUAT * part, part), repeat)
        for tile in range(padded // LANES):
            at = slice(tile * LANES, (tile + 1) * LANES)
            rows = [rows_ref[place, :, at][None] for place in range(QUAT * QUAT)]
            for chunk in range(part // 16):
                spread = [
                    spread_ref[slot, i * part + chunk * 16 : i * part + (chunk + 1) * 16, at]
                    for i in range(QUAT)
                ]
                spread = [value.reshape(2, 8, LANES) for value in spread]
                for a in range(QUAT):
                    total = spread[0] * rows[a]
                    for i in range(1, QUAT):
                        total = total + spread[i] * rows[i * QUAT + a]
                    start = a * part + chunk * 16
                    store(tile, slice(start, start + 16), total.reshape(16, LANES).astype(BF16))

    def store_plain(out):
        def store(tile, rows, value):
            width = min(LANES, channels - tile * LANES)
            out[rows, tile * LANES : tile * LANES + width] = value[:, :width]

        return store

    def store_heads(which):
        def store(tile, rows, value):
            if tile * LANES < full:
                at, low, high = which * full + tile * LANES, 0, LANES
            else:
                at, low = 3 * full + which // 2 * LANES, which % 2 * tail
                high = LANES if which == 2 else low + tail
            qkv_out[rows, at + low : at + high] = value[:, low:high]

        return store

    copies[1].wait()
    for tap in range(9):
        square(tap % 2, conv_ref[tap], store_plain(mix_out.at[tap]))
    copies[2].wait()
    square(1, skip_ref[...], store_plain(mix_out.at[9]))

    for copy in copies[3:10]:
        copy.wait()
    half = channels // 2
    lane = lax.broadcasted_iota(jnp.int32, (8, channels), 1)
    place = jnp.where(lane < half, lane, lane - half).astype(F32)
    frequency = jnp.exp(-math.log(10000.0) * place / half)
    for batch in range(term_out.shape[0]):
        angles = time_ref[batch].astype(F32) * frequency
        features = jnp.where(lane < half, jnp.cos(angles), jnp.sin(angles)).astype(BF16)
        term_out[batch] = dot(features, proj_ref[...])
    meta_out[0] = flag_ref[0]
    meta_out[1] = offset_ref[0]
    for copy in copies[10:]:
        copy.wait()

    @pl.when(flag_ref[0] == 1)
    def _():
        for which in range(3):
            square(which % 2, attn_ref[which], store_heads(which))
        square(1, attn_ref[3], store_plain(out_out))

        def store_wide(out, place, rows, value):
            out[rows, place * full : (place + 1) * full] = value[:, :full].astype(BF16)
            at, low = QUAT * full + place // 2 * LANES, place % 2 * tail
            half_tile = value[:, full + low : full + low + tail].astype(BF16)
            out[rows, at + low : at + low + tail] = half_tile

        def widen(value):
            value = value.astype(F32)
            return jnp.concatenate([value, value[:, full:]], axis=1)

        def wide_step(chunk, carry):
            start = pl.multiple_of(chunk * 16, 16)
            ups = [widen(up_ref[i, pl.ds(start, 16), :]) for i in range(QUAT)]
            downs = [widen(down_ref[i, pl.ds(start, 16), :]) for i in range(QUAT)]
            for a in range(QUAT):
                rows = pl.ds(pl.multiple_of(a * part + start, 16), 16)
                for b, value in enumerate(block_row(ups, a)):
                    store_wide(up_out, b, rows, value)
            for b in range(QUAT):
                rows = pl.ds(pl.multiple_of(b * part + start, 16), 16)
                for a in range(QUAT):
                    total = downs[0] * rule(0, a, b)
                    for i in range(1, QUAT):
                        total = total + downs[i] * rule(i, a, b)
                    store_wide(down_out, a, rows, total)
            return carry

        lax.fori_loop(0, part // 16, wide_step, 0)


def section_weights(
    rule, timesteps, flag, offset, scales, gains, conv, attn, up, down, skip, proj, hidden
):
    channels = proj.shape[0]
    padded = channels // LANES * LANES + LANES
    wide = up.shape[-1]
    operands = (
        rule, timesteps, flag, offset, scales, gains, conv, attn, up, down, skip, proj, hidden,
    )
    return pl.pallas_call(
        weights_kernel,
        out_shape=(
            pltpu.VMEM((10, channels, channels), BF16),
            pltpu.VMEM((channels, 8 * LANES), BF16),
            pltpu.VMEM((channels, channels), BF16),
            pltpu.VMEM((channels, QUAT * wide), BF16),
            pltpu.VMEM((channels, QUAT * wide), BF16),
            pltpu.VMEM((hidden.shape[0], 8, channels), F32),
            pltpu.VMEM(gains.shape, F32),
            pltpu.SMEM((2,), jnp.int32),
            pltpu.SMEM(scales.shape, F32),
            pltpu.VMEM(hidden.shape, BF16),
        ),
        in_specs=[HBM] * len(operands),
        out_specs=(VMEM,) * 7 + (SMEM,) * 2 + (VMEM,),
        scratch_shapes=[
            pltpu.SMEM(rule.shape, F32),
            pltpu.SMEM(timesteps.shape, jnp.int32),
            pltpu.SMEM((1,), jnp.int32),
            pltpu.SMEM((1,), jnp.int32),
        ]
        + [pltpu.VMEM(array.shape, BF16) for array in (conv, attn, up, down, skip, proj)]
        + [
            pltpu.VMEM((QUAT * QUAT, 8, padded), F32),
            pltpu.VMEM((2, channels, padded), F32),
            pltpu.SemaphoreType.DMA((len(operands),)),
        ],
        compiler_params=pltpu.CompilerParams(vmem_limit_bytes=12 * MIB),
        name="weights",
    )(*[in_hbm(v) if v.size > 1 else v for v in operands])


def is_active(tick, batches):
    batch = tick - lax.axis_index("segment")
    return (batch >= 0) & (batch < batches)


def shift_columns(normed, columns):
    total = normed.shape[0]
    col = lax.rem(lax.broadcasted_iota(jnp.int32, (total, 1), 0), columns)
    left = jnp.where(col == 0, 0.0, pltpu.roll(normed, 1, 0)).astype(BF16)
    right = jnp.where(col == columns - 1, 0.0, pltpu.roll(normed, total - 1, 0)).astype(BF16)
    return [left, normed.astype(BF16), right]


def inner_kernel(columns, tick, batches, with_skip, *refs):
    if tick is None:
        tick_ref, *refs = refs
        tick = tick_ref[0]
    if with_skip:
        z_ref, *refs = refs
    x_ref, mix_ref, term_ref, gain_ref, sum_ref = refs
    tokens, channels = x_ref.shape

    @pl.when(is_active(tick, batches))
    def _():
        shifted = shift_columns(rms(x_ref[...].astype(F32), gain_ref[0]), columns)
        edge = jnp.zeros((columns, channels), BF16)
        hidden = jnp.broadcast_to(term_ref[0:1, :], (tokens, channels))
        if with_skip:
            hidden = hidden + dot(z_ref[...], mix_ref[9])
        for b in range(3):
            hidden = hidden + dot(shifted[b], mix_ref[3 + b])
        for b in range(3):
            rows = jnp.concatenate([edge, shifted[b][: tokens - columns]], axis=0)
            hidden = hidden + dot(rows, mix_ref[b])
        for b in range(3):
            rows = jnp.concatenate([shifted[b][columns:], edge], axis=0)
            hidden = hidden + dot(rows, mix_ref[6 + b])
        sum_ref[...] = hidden


def attention(normed, qkv_ref, scales_ref, offset, columns):
    tokens = normed.shape[0]
    projected = dot(normed, qkv_ref[...]).astype(BF16)
    tiles = [projected[:, t * LANES : (t + 1) * LANES] for t in range(8)]
    lane = lax.broadcasted_iota(jnp.int32, (tokens, LANES), 1)
    left = lane < HEAD

    groups = lax.broadcasted_iota(jnp.int32, (LANES, LANES), 0) // HEAD
    groups = groups == lax.broadcasted_iota(jnp.int32, (LANES, LANES), 1) // HEAD
    groups = jnp.where(groups, 1.0, 0.0).astype(BF16)
    scaled = [tiles[t].astype(F32) for t in (0, 1, 2, 3, 6)]
    squares = jnp.concatenate([(v * v).astype(BF16) for v in scaled], axis=0)
    inverse = lax.rsqrt(dot(squares, groups) + COS_EPSILON)
    factors = [
        jnp.where(left, scales_ref[0, 0], scales_ref[0, 1]),
        jnp.where(left, scales_ref[0, 2], scales_ref[0, 3]),
        None,
        None,
        jnp.where(left, scales_ref[0, 4], 1.0),
    ]
    units = []
    for place, (value, factor) in enumerate(zip(scaled, factors)):
        norm = inverse[place * tokens : (place + 1) * tokens]
        units.append(value * (norm if factor is None else norm * factor))
    last_key = pltpu.roll(units[4], HEAD, 1).astype(BF16)
    units = [value.astype(BF16) for value in units]

    def window(index):
        return lax.rem(lax.rem(index, columns) - offset + columns, columns) // WIN

    row_window = window(lax.broadcasted_iota(jnp.int32, (tokens, 1), 0))
    same = row_window == window(lax.broadcasted_iota(jnp.int32, (1, tokens), 1))
    zero, one = jnp.zeros((), BF16), jnp.ones((), BF16)

    def weights(query, keys):
        return jnp.where(same, jnp.exp(dot_t(query, keys)), 0.0).astype(BF16)

    mixed = []
    for t in range(2):
        even = weights(jnp.where(left, units[t], zero), units[2 + t])
        odd = weights(jnp.where(left, zero, units[t]), units[2 + t])
        even = dot(even, jnp.where(left, tiles[4 + t], one))
        odd = dot(odd, jnp.where(left, one, tiles[4 + t]))
        sums = pltpu.roll(jnp.where(left, odd, even), HEAD, 1)
        mixed.append((jnp.where(left, even, odd) / sums).astype(BF16))
    even = weights(jnp.where(left, units[4], zero), last_key)
    even = dot(even, jnp.where(left, tiles[7], one))
    mixed.append((even / pltpu.roll(even, HEAD, 1)).astype(BF16)[:, :HEAD])
    return jnp.concatenate(mixed, axis=1)


def outer_kernel(columns, tick, batches, *refs):
    if tick is None:
        tick_ref, *refs = refs
        tick = tick_ref[0]
    (
        meta_ref, scales_ref, x_ref, sum_ref, low_ref, high_ref, prev_ref, mix_ref, qkv_ref,
        proj_ref, up_ref, down_ref, gain_ref, out_ref, first_ref, last_ref,
    ) = refs
    tokens, channels = x_ref.shape
    active = is_active(tick, batches)

    def write(x3):
        value = x3.astype(BF16)
        out_ref[...] = value
        first_ref[...] = value[:columns]
        last_ref[...] = value[tokens - columns :]

    @pl.when(jnp.logical_not(active))
    def _():
        out_ref[...] = prev_ref[...]

    @pl.when(active)
    def _():
        gain = [gain_ref[row] for row in range(3)]
        below = low_ref.shape[0] - columns
        low = shift_columns(rms(low_ref[below:].astype(F32), gain[0]), columns)
        high = shift_columns(rms(high_ref[:columns].astype(F32), gain[0]), columns)
        top = sum_ref[:columns]
        bottom = sum_ref[tokens - columns :]
        for b in range(3):
            top = top + dot(low[b], mix_ref[b])
            bottom = bottom + dot(high[b], mix_ref[6 + b])
        hidden = jnp.concatenate([top, sum_ref[columns : tokens - columns], bottom], axis=0)
        x1 = x_ref[...].astype(F32) + silu(hidden)
        has_block, offset = meta_ref[0], meta_ref[1]

        @pl.when(has_block != 1)
        def _():
            write(x1)

        @pl.when(has_block == 1)
        def _():
            n2 = rms(x1, gain[1]).astype(BF16)
            heads = attention(n2, qkv_ref, scales_ref, offset, columns)
            x2 = x1 + dot(heads, proj_ref[...])
            n3 = rms(x2, gain[2]).astype(BF16)
            act = silu(dot(n3, up_ref[...])).astype(BF16)
            x3 = x2 + dot_t(act, down_ref[...])
            write(x3)


def run_inner(columns, tick, batches, x, z, mix, term, gains):
    static = isinstance(tick, int)
    with_skip = z is not None
    operands = [z] if with_skip else []
    operands += [x, in_vmem(mix), term, in_vmem(gains)]
    specs = [VMEM] * len(operands)
    if not static:
        operands, specs = [tick] + operands, [SMEM] + specs
    return pl.pallas_call(
        functools.partial(inner_kernel, columns, tick if static else None, batches, with_skip),
        out_shape=pltpu.VMEM(x.shape, F32),
        in_specs=specs,
        out_specs=VMEM,
        compiler_params=pltpu.CompilerParams(vmem_limit_bytes=8 * MIB),
        name="inner",
    )(*operands)


def run_outer(columns, tick, batches, x, total, low, high, prev, weights):
    static = isinstance(tick, int)
    mix, qkv, proj, up, down, gains, meta, scales = weights
    operands = [in_smem(meta), in_smem(scales), x, in_vmem(total), low, high, prev]
    operands += [in_vmem(w) for w in (mix, qkv, proj, up, down, gains)]
    specs = [SMEM] * 2 + [VMEM] * (len(operands) - 2)
    if not static:
        operands, specs = [tick] + operands, [SMEM] + specs
    edge = jax.ShapeDtypeStruct((columns, x.shape[1]), BF16)
    return pl.pallas_call(
        functools.partial(outer_kernel, columns, tick if static else None, batches),
        out_shape=(jax.ShapeDtypeStruct(x.shape, BF16), edge, edge),
        in_specs=specs,
        out_specs=(VMEM,) * 3,
        compiler_params=pltpu.CompilerParams(vmem_limit_bytes=8 * MIB),
        name="outer",
    )(*operands)


def shards(
    hidden, timesteps, rule_matrices, conv_factors, time_proj, skip_factors, attn_factors,
    up_factors, down_factors, norm_gains, head_scales, has_block, offsets,
):
    segments = lax.axis_size("segment")
    row_parts = lax.axis_size("rows")
    half = segments // 2
    segment = lax.axis_index("segment")
    batches, height, columns, channels = hidden.shape
    tokens = height * columns
    axes = ("segment", "rows")

    def pairs(sources, step, turn):
        return [
            (s * row_parts + r, (s + step) * row_parts + r + turn)
            for s in sources
            for r in range(row_parts)
            if 0 <= s + step < segments and 0 <= r + turn < row_parts
        ]

    def pass_on(value, sources, step, turn):
        links = pairs(sources, step, turn)
        if not links:
            return jnp.zeros_like(value)
        return lax.ppermute(value, axes, links)

    flat = hidden.reshape(batches, tokens, channels)
    near, far = min(1, segments - 1), min(2, segments - 1)
    low0 = pass_on(flat, [near], -near, 1)
    high0 = pass_on(flat, [far], -far, -1)
    mix, qkv, proj, up, down, terms, gains, meta, scales, flat = section_weights(
        rule_matrices[0], timesteps, has_block, offsets, head_scales,
        jnp.transpose(norm_gains, (1, 0, 2)), conv_factors[0], attn_factors[0], up_factors[0],
        jnp.transpose(down_factors[0], (0, 2, 1)), skip_factors[0], time_proj[0], flat,
    )
    weights = (mix, qkv, proj, up, down, gains, meta, scales)

    def section(tick, x, low, high, z, prev, term):
        total = run_inner(columns, tick, batches, x, z, mix, term, gains)
        return run_outer(columns, tick, batches, x, total, low, high, prev, weights)

    def edges_on(out, first, last, sources):
        main = pass_on(out, sources, 1, 0)
        low = pass_on(last, sources, 1, 1)
        high = pass_on(first, sources, 1, -1)
        return main, low, high

    if batches == 1:
        x, low, high = flat[0], low0[0], high0[0]
        out = flat[0]
        skips = []
        for tick in range(segments):
            z = skips[tick - half] if tick >= half else None
            out, first, last = section(tick, x, low, high, z, out, terms[0])
            if tick + 1 < segments:
                x, low, high = edges_on(out, first, last, [tick])
                skips.append(pass_on(out, [tick], half, 0) if tick + half < segments else None)
        return out.reshape(1, batches, height, columns, channels)

    def pick(array, slot):
        return lax.dynamic_index_in_dim(array, slot, 0, keepdims=False)

    def tick_step(tick, state):
        states, received, skip_buffer = state
        slot = jnp.clip(tick - segment, 0, batches - 1)
        own = pick(flat, slot), pick(low0, slot)[tokens - columns :], pick(high0, slot)[:columns]
        x, low, high = [jnp.where(segment == 0, f, r) for f, r in zip(own, received)]
        out, first, last = section(
            jnp.reshape(tick, (1,)), x, low, high, pick(skip_buffer, slot), pick(states, slot),
            pick(terms, slot),
        )
        states = lax.dynamic_update_index_in_dim(states, out, slot, 0)
        passed = edges_on(out, first, last, range(segments))
        arrived = pass_on(out, range(segments), half, 0)
        partner = tick - segment + half
        fits = (segment >= half) & (partner >= 0) & (partner < batches)
        partner_slot = jnp.clip(partner, 0, batches - 1)
        kept = pick(skip_buffer, partner_slot)
        skip_buffer = lax.dynamic_update_index_in_dim(
            skip_buffer, jnp.where(fits, arrived, kept), partner_slot, 0
        )
        return states, passed, skip_buffer

    edge = jnp.zeros((columns, channels), BF16)
    initial = (jnp.zeros_like(flat), (jnp.zeros_like(flat[0]), edge, edge), jnp.zeros_like(flat))
    states = lax.fori_loop(0, batches + segments - 1, tick_step, initial)[0]
    return states.reshape(1, batches, height, columns, channels)


def solution(mesh):
    return jax.shard_map(
        shards,
        mesh=mesh,
        in_specs=(
            P("groups", "rows", None, None),
            P("groups"),
            P("segment", None, None, None),
            P("segment", None, None, None, None),
            P("segment", None, None),
            P("segment", None, None, None),
            P("segment", None, None, None, None),
            P("segment", None, None, None),
            P("segment", None, None, None),
            P("segment", None, None),
            P("segment", None),
            P("segment"),
            P("segment"),
        ),
        out_specs=P("segment", "groups", "rows", None, None),
        check_vma=False,
    )
```

```python
import functools
import math

import jax
import jax.numpy as jnp
from jax import lax
from jax.experimental import pallas as pl
from jax.experimental.pallas import tpu as pltpu
from jax.sharding import PartitionSpec as P

HEAD = 64
WIN = 8
QUAT = 4

EPSILON = 1e-05
COS_EPSILON = 1e-06

F32 = jnp.float32
BF16 = jnp.bfloat16
MIB = 1024 * 1024
LANES = 128

VMEM = pl.BlockSpec(memory_space=pltpu.VMEM)
SMEM = pl.BlockSpec(memory_space=pltpu.SMEM)
HBM = pl.BlockSpec(memory_space=pltpu.HBM)


def in_vmem(value):
    return pltpu.with_memory_space_constraint(value, pltpu.VMEM)


def in_smem(value):
    return pltpu.with_memory_space_constraint(value, pltpu.SMEM)


def in_hbm(value):
    return pltpu.with_memory_space_constraint(value, pltpu.HBM)


def dot(left, right):
    return jnp.dot(left, right, preferred_element_type=F32)


def dot_t(left, right):
    return lax.dot_general(left, right, (((1,), (1,)), ((), ())), preferred_element_type=F32)


def rms(values, gain_row):
    mean_square = jnp.mean(values * values, axis=-1, keepdims=True)
    return values * lax.rsqrt(mean_square + EPSILON) * gain_row


def silu(values):
    return values / (1.0 + jnp.exp(-values))


def weights_kernel(
    first_skip, rule_hbm, time_hbm, flag_hbm, offset_hbm, scale_hbm, gain_hbm,
    conv_hbm, attn_hbm, up_hbm, down_hbm, skip_hbm, proj_hbm, hidden_hbm,
    mix_out, qkv_out, out_out, up_out, down_out, term_out, gain_out, meta_out, scale_out,
    hidden_out,
    rule_ref, time_ref, flag_ref, offset_ref, conv_ref, attn_ref, up_ref, down_ref,
    skip_ref, proj_ref, rows_ref, sems,
):
    sources = [
        rule_hbm, conv_hbm, skip_hbm, time_hbm, proj_hbm, flag_hbm, offset_hbm, scale_hbm,
        gain_hbm, hidden_hbm, attn_hbm, up_hbm, down_hbm,
    ]
    targets = [
        rule_ref, conv_ref, skip_ref, time_ref, proj_ref, flag_ref, offset_ref, scale_out,
        gain_out, hidden_out, attn_ref, up_ref, down_ref,
    ]
    copies = [
        pltpu.make_async_copy(source, target, sems.at[place])
        for place, (source, target) in enumerate(zip(sources, targets))
    ]
    for copy in copies:
        copy.start()
    part = conv_ref.shape[-1]

    def rule(i, a, b):
        return rule_ref[i, a, b]

    def block_row(factors, a):
        blocks = []
        for b in range(QUAT):
            total = factors[0] * rule(0, a, b)
            for i in range(1, QUAT):
                total = total + factors[i] * rule(i, a, b)
            blocks.append(total)
        return blocks

    channels = proj_ref.shape[0]
    tail = channels % LANES
    full = channels - tail
    padded = full + LANES

    def channel_of(lane):
        return jnp.where(lane < channels, lane, lane - tail)

    lanes = channel_of(lax.broadcasted_iota(jnp.int32, (part, padded), 1))
    ones = lax.rem(lanes, part) == lax.broadcasted_iota(jnp.int32, (part, padded), 0)
    repeat = jnp.where(ones, 1.0, 0.0).astype(BF16)
    copies[0].wait()
    block = channel_of(lax.broadcasted_iota(jnp.int32, (8, padded), 1)) // part
    for i in range(QUAT):
        for a in range(QUAT):
            row = jnp.where(block == 0, rule(i, a, 0), rule(i, a, 1))
            row = jnp.where(block == 2, rule(i, a, 2), row)
            rows_ref[i * QUAT + a] = jnp.where(block == 3, rule(i, a, 3), row)

    def square(factors, store):
        stacked = factors.reshape(QUAT * part, part)
        for tile in range(padded // LANES):
            at = slice(tile * LANES, (tile + 1) * LANES)
            rows = [rows_ref[place, :, at][None] for place in range(QUAT * QUAT)]
            whole = dot(stacked, repeat[:, at])
            for chunk in range(part // 16):
                spread = [
                    whole[i * part + chunk * 16 : i * part + (chunk + 1) * 16]
                    for i in range(QUAT)
                ]
                spread = [value.reshape(2, 8, LANES) for value in spread]
                for a in range(QUAT):
                    total = spread[0] * rows[a]
                    for i in range(1, QUAT):
                        total = total + spread[i] * rows[i * QUAT + a]
                    start = a * part + chunk * 16
                    store(tile, slice(start, start + 16), total.reshape(16, LANES).astype(BF16))

    def store_plain(out):
        def store(tile, rows, value):
            width = min(LANES, channels - tile * LANES)
            out[rows, tile * LANES : tile * LANES + width] = value[:, :width]

        return store

    def store_heads(which):
        def store(tile, rows, value):
            if tile * LANES < full:
                at, low, high = which * full + tile * LANES, 0, LANES
            else:
                at, low = 3 * full + which // 2 * LANES, which % 2 * tail
                high = LANES if which == 2 else low + tail
            qkv_out[rows, at + low : at + high] = value[:, low:high]

        return store

    copies[1].wait()
    for tap in range(9):
        square(conv_ref[tap], store_plain(mix_out.at[tap]))
    copies[2].wait()

    @pl.when(lax.axis_index("segment") >= first_skip)
    def _():
        square(skip_ref[...], store_plain(mix_out.at[9]))

    for copy in copies[3:10]:
        copy.wait()
    half = channels // 2
    lane = lax.broadcasted_iota(jnp.int32, (8, channels), 1)
    place = jnp.where(lane < half, lane, lane - half).astype(F32)
    frequency = jnp.exp(-math.log(10000.0) * place / half)
    for batch in range(term_out.shape[0]):
        angles = time_ref[batch].astype(F32) * frequency
        features = jnp.where(lane < half, jnp.cos(angles), jnp.sin(angles)).astype(BF16)
        term_out[batch] = dot(features, proj_ref[...])
    meta_out[0] = flag_ref[0]
    meta_out[1] = offset_ref[0]
    for copy in copies[10:]:
        copy.wait()

    @pl.when(flag_ref[0] == 1)
    def _():
        for which in range(3):
            square(attn_ref[which], store_heads(which))
        square(attn_ref[3], store_plain(out_out))

        def store_wide(out, place, rows, value):
            out[rows, place * full : (place + 1) * full] = value[:, :full].astype(BF16)
            at, low = QUAT * full + place // 2 * LANES, place % 2 * tail
            half_tile = value[:, full + low : full + low + tail].astype(BF16)
            out[rows, at + low : at + low + tail] = half_tile

        def widen(value):
            value = value.astype(F32)
            return jnp.concatenate([value, value[:, full:]], axis=1)

        def wide_step(chunk, carry):
            start = pl.multiple_of(chunk * 16, 16)
            ups = [widen(up_ref[i, pl.ds(start, 16), :]) for i in range(QUAT)]
            downs = [widen(down_ref[i, pl.ds(start, 16), :]) for i in range(QUAT)]
            for a in range(QUAT):
                rows = pl.ds(pl.multiple_of(a * part + start, 16), 16)
                for b, value in enumerate(block_row(ups, a)):
                    store_wide(up_out, b, rows, value)
            for b in range(QUAT):
                rows = pl.ds(pl.multiple_of(b * part + start, 16), 16)
                for a in range(QUAT):
                    total = downs[0] * rule(0, a, b)
                    for i in range(1, QUAT):
                        total = total + downs[i] * rule(i, a, b)
                    store_wide(down_out, a, rows, total)
            return carry

        lax.fori_loop(0, part // 16, wide_step, 0)


def section_weights(
    first_skip, rule, timesteps, flag, offset, scales, gains, conv, attn, up, down, skip, proj, hidden
):
    channels = proj.shape[0]
    padded = channels // LANES * LANES + LANES
    wide = up.shape[-1]
    operands = (
        rule, timesteps, flag, offset, scales, gains, conv, attn, up, down, skip, proj, hidden,
    )
    return pl.pallas_call(
        functools.partial(weights_kernel, first_skip),
        out_shape=(
            pltpu.VMEM((10, channels, channels), BF16),
            pltpu.VMEM((channels, 8 * LANES), BF16),
            pltpu.VMEM((channels, channels), BF16),
            pltpu.VMEM((channels, QUAT * wide), BF16),
            pltpu.VMEM((channels, QUAT * wide), BF16),
            pltpu.VMEM((hidden.shape[0], 8, channels), F32),
            pltpu.VMEM(gains.shape, F32),
            pltpu.SMEM((2,), jnp.int32),
            pltpu.SMEM(scales.shape, F32),
            pltpu.VMEM(hidden.shape, BF16),
        ),
        in_specs=[HBM] * len(operands),
        out_specs=(VMEM,) * 7 + (SMEM,) * 2 + (VMEM,),
        scratch_shapes=[
            pltpu.SMEM(rule.shape, F32),
            pltpu.SMEM(timesteps.shape, jnp.int32),
            pltpu.SMEM((1,), jnp.int32),
            pltpu.SMEM((1,), jnp.int32),
        ]
        + [pltpu.VMEM(array.shape, BF16) for array in (conv, attn, up, down, skip, proj)]
        + [
            pltpu.VMEM((QUAT * QUAT, 8, padded), F32),
            pltpu.SemaphoreType.DMA((len(operands),)),
        ],
        compiler_params=pltpu.CompilerParams(vmem_limit_bytes=12 * MIB),
        name="weights",
    )(*[in_hbm(v) if v.size > 1 else v for v in operands])


def is_active(tick, batches):
    batch = tick - lax.axis_index("segment")
    return (batch >= 0) & (batch < batches)


def shift_columns(normed, columns):
    total = normed.shape[0]
    col = lax.rem(lax.broadcasted_iota(jnp.int32, (total, 1), 0), columns)
    left = jnp.where(col == 0, 0.0, pltpu.roll(normed, 1, 0)).astype(BF16)
    right = jnp.where(col == columns - 1, 0.0, pltpu.roll(normed, total - 1, 0)).astype(BF16)
    return [left, normed.astype(BF16), right]


def inner_kernel(columns, tick, batches, with_skip, *refs):
    if tick is None:
        tick_ref, *refs = refs
        tick = tick_ref[0]
    if with_skip:
        z_ref, *refs = refs
    x_ref, mix_ref, term_ref, gain_ref, sum_ref = refs
    tokens, channels = x_ref.shape

    @pl.when(is_active(tick, batches))
    def _():
        shifted = shift_columns(rms(x_ref[...].astype(F32), gain_ref[0]), columns)
        edge = jnp.zeros((columns, channels), BF16)
        hidden = jnp.broadcast_to(term_ref[0:1, :], (tokens, channels))
        if with_skip:
            hidden = hidden + dot(z_ref[...], mix_ref[9])
        for b in range(3):
            hidden = hidden + dot(shifted[b], mix_ref[3 + b])
        for b in range(3):
            rows = jnp.concatenate([edge, shifted[b][: tokens - columns]], axis=0)
            hidden = hidden + dot(rows, mix_ref[b])
        for b in range(3):
            rows = jnp.concatenate([shifted[b][columns:], edge], axis=0)
            hidden = hidden + dot(rows, mix_ref[6 + b])
        sum_ref[...] = hidden


def attention(normed, qkv_ref, scales_ref, offset, columns):
    tokens = normed.shape[0]
    projected = dot(normed, qkv_ref[...]).astype(BF16)
    tiles = [projected[:, t * LANES : (t + 1) * LANES] for t in range(8)]
    lane = lax.broadcasted_iota(jnp.int32, (tokens, LANES), 1)
    left = lane < HEAD

    groups = lax.broadcasted_iota(jnp.int32, (LANES, LANES), 0) // HEAD
    groups = groups == lax.broadcasted_iota(jnp.int32, (LANES, LANES), 1) // HEAD
    groups = jnp.where(groups, 1.0, 0.0).astype(BF16)
    scaled = [tiles[t].astype(F32) for t in (0, 1, 2, 3, 6)]
    squares = jnp.concatenate([(v * v).astype(BF16) for v in scaled], axis=0)
    inverse = lax.rsqrt(dot(squares, groups) + COS_EPSILON)
    factors = [
        jnp.where(left, scales_ref[0, 0], scales_ref[0, 1]),
        jnp.where(left, scales_ref[0, 2], scales_ref[0, 3]),
        None,
        None,
        jnp.where(left, scales_ref[0, 4], 1.0),
    ]
    units = []
    for place, (value, factor) in enumerate(zip(scaled, factors)):
        norm = inverse[place * tokens : (place + 1) * tokens]
        units.append(value * (norm if factor is None else norm * factor))
    last_key = pltpu.roll(units[4], HEAD, 1).astype(BF16)
    units = [value.astype(BF16) for value in units]

    def window(index):
        return lax.rem(lax.rem(index, columns) - offset + columns, columns) // WIN

    row_window = window(lax.broadcasted_iota(jnp.int32, (tokens, 1), 0))
    same = row_window == window(lax.broadcasted_iota(jnp.int32, (1, tokens), 1))
    zero, one = jnp.zeros((), BF16), jnp.ones((), BF16)

    def weights(query, keys):
        return jnp.where(same, jnp.exp(dot_t(query, keys)), 0.0).astype(BF16)

    mixed = []
    for t in range(2):
        even = weights(jnp.where(left, units[t], zero), units[2 + t])
        odd = weights(jnp.where(left, zero, units[t]), units[2 + t])
        even = dot(even, jnp.where(left, tiles[4 + t], one))
        odd = dot(odd, jnp.where(left, one, tiles[4 + t]))
        sums = pltpu.roll(jnp.where(left, odd, even), HEAD, 1)
        mixed.append((jnp.where(left, even, odd) / sums).astype(BF16))
    even = weights(jnp.where(left, units[4], zero), last_key)
    even = dot(even, jnp.where(left, tiles[7], one))
    mixed.append((even / pltpu.roll(even, HEAD, 1)).astype(BF16)[:, :HEAD])
    return jnp.concatenate(mixed, axis=1)


def outer_kernel(columns, tick, batches, *refs):
    if tick is None:
        tick_ref, *refs = refs
        tick = tick_ref[0]
    (
        meta_ref, scales_ref, x_ref, sum_ref, low_ref, high_ref, prev_ref, mix_ref, qkv_ref,
        proj_ref, up_ref, down_ref, gain_ref, out_ref, first_ref, last_ref,
    ) = refs
    tokens, channels = x_ref.shape
    active = is_active(tick, batches)

    def write(x3):
        value = x3.astype(BF16)
        out_ref[...] = value
        first_ref[...] = value[:columns]
        last_ref[...] = value[tokens - columns :]

    @pl.when(jnp.logical_not(active))
    def _():
        out_ref[...] = prev_ref[...]

    @pl.when(active)
    def _():
        gain = [gain_ref[row] for row in range(3)]
        below = low_ref.shape[0] - columns
        low = shift_columns(rms(low_ref[below:].astype(F32), gain[0]), columns)
        high = shift_columns(rms(high_ref[:columns].astype(F32), gain[0]), columns)
        top = sum_ref[:columns]
        bottom = sum_ref[tokens - columns :]
        for b in range(3):
            top = top + dot(low[b], mix_ref[b])
            bottom = bottom + dot(high[b], mix_ref[6 + b])
        hidden = jnp.concatenate([top, sum_ref[columns : tokens - columns], bottom], axis=0)
        x1 = x_ref[...].astype(F32) + silu(hidden)
        has_block, offset = meta_ref[0], meta_ref[1]

        @pl.when(has_block != 1)
        def _():
            write(x1)

        @pl.when(has_block == 1)
        def _():
            n2 = rms(x1, gain[1]).astype(BF16)
            heads = attention(n2, qkv_ref, scales_ref, offset, columns)
            x2 = x1 + dot(heads, proj_ref[...])
            n3 = rms(x2, gain[2]).astype(BF16)
            act = silu(dot(n3, up_ref[...])).astype(BF16)
            x3 = x2 + dot_t(act, down_ref[...])
            write(x3)


def run_inner(columns, tick, batches, x, z, mix, term, gains):
    static = isinstance(tick, int)
    with_skip = z is not None
    operands = [z] if with_skip else []
    operands += [x, in_vmem(mix), term, in_vmem(gains)]
    specs = [VMEM] * len(operands)
    if not static:
        operands, specs = [tick] + operands, [SMEM] + specs
    return pl.pallas_call(
        functools.partial(inner_kernel, columns, tick if static else None, batches, with_skip),
        out_shape=pltpu.VMEM(x.shape, F32),
        in_specs=specs,
        out_specs=VMEM,
        compiler_params=pltpu.CompilerParams(vmem_limit_bytes=8 * MIB),
        name="inner",
    )(*operands)


def run_outer(columns, tick, batches, x, total, low, high, prev, weights):
    static = isinstance(tick, int)
    mix, qkv, proj, up, down, gains, meta, scales = weights
    operands = [in_smem(meta), in_smem(scales), x, in_vmem(total), low, high, prev]
    operands += [in_vmem(w) for w in (mix, qkv, proj, up, down, gains)]
    specs = [SMEM] * 2 + [VMEM] * (len(operands) - 2)
    if not static:
        operands, specs = [tick] + operands, [SMEM] + specs
    edge = jax.ShapeDtypeStruct((columns, x.shape[1]), BF16)
    return pl.pallas_call(
        functools.partial(outer_kernel, columns, tick if static else None, batches),
        out_shape=(jax.ShapeDtypeStruct(x.shape, BF16), edge, edge),
        in_specs=specs,
        out_specs=(VMEM,) * 3,
        compiler_params=pltpu.CompilerParams(vmem_limit_bytes=8 * MIB),
        name="outer",
    )(*operands)


def shards(
    hidden, timesteps, rule_matrices, conv_factors, time_proj, skip_factors, attn_factors,
    up_factors, down_factors, norm_gains, head_scales, has_block, offsets,
):
    segments = lax.axis_size("segment")
    row_parts = lax.axis_size("rows")
    half = segments // 2
    segment = lax.axis_index("segment")
    batches, height, columns, channels = hidden.shape
    tokens = height * columns
    axes = ("segment", "rows")

    def pairs(sources, step, turn):
        return [
            (s * row_parts + r, (s + step) * row_parts + r + turn)
            for s in sources
            for r in range(row_parts)
            if 0 <= s + step < segments and 0 <= r + turn < row_parts
        ]

    def pass_on(value, sources, step, turn):
        links = pairs(sources, step, turn)
        if not links:
            return jnp.zeros_like(value)
        return lax.ppermute(value, axes, links)

    flat = hidden.reshape(batches, tokens, channels)
    near, far = min(1, segments - 1), min(2, segments - 1)
    low0 = pass_on(flat, [near], -near, 1)
    high0 = pass_on(flat, [far], -far, -1)
    mix, qkv, proj, up, down, terms, gains, meta, scales, flat = section_weights(
        half if batches == 1 else 0,
        rule_matrices[0], timesteps, has_block, offsets, head_scales,
        jnp.transpose(norm_gains, (1, 0, 2)), conv_factors[0], attn_factors[0], up_factors[0],
        jnp.transpose(down_factors[0], (0, 2, 1)), skip_factors[0], time_proj[0], flat,
    )
    weights = (mix, qkv, proj, up, down, gains, meta, scales)

    def section(tick, x, low, high, z, prev, term):
        total = run_inner(columns, tick, batches, x, z, mix, term, gains)
        return run_outer(columns, tick, batches, x, total, low, high, prev, weights)

    def edges_on(out, first, last, sources):
        main = pass_on(out, sources, 1, 0)
        low = pass_on(last, sources, 1, 1)
        high = pass_on(first, sources, 1, -1)
        return main, low, high

    if batches == 1:
        x, low, high = flat[0], low0[0], high0[0]
        out = flat[0]
        skips = []
        for tick in range(segments):
            z = skips[tick - half] if tick >= half else None
            out, first, last = section(tick, x, low, high, z, out, terms[0])
            if tick + 1 < segments:
                x, low, high = edges_on(out, first, last, [tick])
                skips.append(pass_on(out, [tick], half, 0) if tick + half < segments else None)
        return out.reshape(1, batches, height, columns, channels)

    def pick(array, slot):
        return lax.dynamic_index_in_dim(array, slot, 0, keepdims=False)

    def tick_step(tick, state):
        states, received, skip_buffer = state
        slot = jnp.clip(tick - segment, 0, batches - 1)
        own = pick(flat, slot), pick(low0, slot)[tokens - columns :], pick(high0, slot)[:columns]
        x, low, high = [jnp.where(segment == 0, f, r) for f, r in zip(own, received)]
        out, first, last = section(
            jnp.reshape(tick, (1,)), x, low, high, pick(skip_buffer, slot), pick(states, slot),
            pick(terms, slot),
        )
        states = lax.dynamic_update_index_in_dim(states, out, slot, 0)
        passed = edges_on(out, first, last, range(segments))
        arrived = pass_on(out, range(segments), half, 0)
        partner = tick - segment + half
        fits = (segment >= half) & (partner >= 0) & (partner < batches)
        partner_slot = jnp.clip(partner, 0, batches - 1)
        kept = pick(skip_buffer, partner_slot)
        skip_buffer = lax.dynamic_update_index_in_dim(
            skip_buffer, jnp.where(fits, arrived, kept), partner_slot, 0
        )
        return states, passed, skip_buffer

    edge = jnp.zeros((columns, channels), BF16)
    initial = (jnp.zeros_like(flat), (jnp.zeros_like(flat[0]), edge, edge), jnp.zeros_like(flat))
    states = lax.fori_loop(0, batches + segments - 1, tick_step, initial)[0]
    return states.reshape(1, batches, height, columns, channels)


def solution(mesh):
    return jax.shard_map(
        shards,
        mesh=mesh,
        in_specs=(
            P("groups", "rows", None, None),
            P("groups"),
            P("segment", None, None, None),
            P("segment", None, None, None, None),
            P("segment", None, None),
            P("segment", None, None, None),
            P("segment", None, None, None, None),
            P("segment", None, None, None),
            P("segment", None, None, None),
            P("segment", None, None),
            P("segment", None),
            P("segment"),
            P("segment"),
        ),
        out_specs=P("segment", "groups", "rows", None, None),
        check_vma=False,
    )
```

```python
import functools
import math

import jax
import jax.numpy as jnp
from jax import lax
from jax.experimental import pallas as pl
from jax.experimental.pallas import tpu as pltpu
from jax.sharding import PartitionSpec as P

HEAD = 64
WIN = 8
QUAT = 4

EPSILON = 1e-05
COS_EPSILON = 1e-06

F32 = jnp.float32
BF16 = jnp.bfloat16
MIB = 1024 * 1024
LANES = 128

VMEM = pl.BlockSpec(memory_space=pltpu.VMEM)
SMEM = pl.BlockSpec(memory_space=pltpu.SMEM)
HBM = pl.BlockSpec(memory_space=pltpu.HBM)


def in_vmem(value):
    return pltpu.with_memory_space_constraint(value, pltpu.VMEM)


def in_smem(value):
    return pltpu.with_memory_space_constraint(value, pltpu.SMEM)


def in_hbm(value):
    return pltpu.with_memory_space_constraint(value, pltpu.HBM)


def dot(left, right):
    return jnp.dot(left, right, preferred_element_type=F32)


def dot_t(left, right):
    return lax.dot_general(left, right, (((1,), (1,)), ((), ())), preferred_element_type=F32)


def rms(values, gain_row):
    mean_square = jnp.mean(values * values, axis=-1, keepdims=True)
    return values * lax.rsqrt(mean_square + EPSILON) * gain_row


def silu(values):
    return values / (1.0 + jnp.exp(-values))


def weights_kernel(
    first_skip, rule_hbm, time_hbm, flag_hbm, offset_hbm, scale_hbm, gain_hbm,
    conv_hbm, attn_hbm, up_hbm, down_hbm, skip_hbm, proj_hbm, hidden_hbm,
    mix_out, qkv_out, out_out, up_out, down_out, term_out, gain_out, meta_out, scale_out,
    hidden_out,
    rule_ref, time_ref, flag_ref, offset_ref, conv_ref, attn_ref, up_ref, down_ref,
    skip_ref, proj_ref, rows_ref, pair_ref, sems,
):
    sources = [
        rule_hbm, conv_hbm, skip_hbm, time_hbm, proj_hbm, flag_hbm, offset_hbm, scale_hbm,
        gain_hbm, hidden_hbm, attn_hbm, up_hbm, down_hbm,
    ]
    targets = [
        rule_ref, conv_ref, skip_ref, time_ref, proj_ref, flag_ref, offset_ref, scale_out,
        gain_out, hidden_out, attn_ref, up_ref, down_ref,
    ]
    copies = [
        pltpu.make_async_copy(source, target, sems.at[place])
        for place, (source, target) in enumerate(zip(sources, targets))
    ]
    for copy in copies:
        copy.start()
    part = conv_ref.shape[-1]

    def rule(i, a, b):
        return rule_ref[i, a, b]

    channels = proj_ref.shape[0]
    tail = channels % LANES
    full = channels - tail
    padded = full + LANES

    def channel_of(lane):
        return jnp.where(lane < channels, lane, lane - tail)

    lanes = channel_of(lax.broadcasted_iota(jnp.int32, (part, padded), 1))
    ones = lax.rem(lanes, part) == lax.broadcasted_iota(jnp.int32, (part, padded), 0)
    repeat = jnp.where(ones, 1.0, 0.0).astype(BF16)
    copies[0].wait()
    block = channel_of(lax.broadcasted_iota(jnp.int32, (8, padded), 1)) // part
    for i in range(QUAT):
        for a in range(QUAT):
            row = jnp.where(block == 0, rule(i, a, 0), rule(i, a, 1))
            row = jnp.where(block == 2, rule(i, a, 2), row)
            rows_ref[i * QUAT + a] = jnp.where(block == 3, rule(i, a, 3), row)
    on_left = lax.broadcasted_iota(jnp.int32, (8, LANES), 1) < tail
    for place in range(QUAT * QUAT // 2):
        left, right = rows_ref[2 * place, :, full:], rows_ref[2 * place + 1, :, full:]
        pair_ref[place] = jnp.where(on_left, left, right)

    def combine(parts, scales):
        total = parts[0] * scales[0]
        for value, scale in zip(parts[1:], scales[1:]):
            total = total + value * scale
        return total

    def square(factors, store, keep_right=False):
        stacked = factors.reshape(QUAT * part, part)
        for tile in range(padded // LANES):
            at = slice(tile * LANES, (tile + 1) * LANES)
            halves = tile * LANES == full
            if halves:
                rows = [pair_ref[place][None] for place in range(QUAT * QUAT // 2)]
            else:
                rows = [rows_ref[place, :, at][None] for place in range(QUAT * QUAT)]
            step = 2 if halves else 1
            groups = QUAT // step
            whole = dot(stacked, repeat[:, at])
            for chunk in range(part // 16):
                spread = [
                    whole[i * part + chunk * 16 : i * part + (chunk + 1) * 16]
                    for i in range(QUAT)
                ]
                spread = [value.reshape(2, 8, LANES) for value in spread]
                for group in range(groups):
                    scales = [rows[i * groups + group] for i in range(QUAT)]
                    total = combine(spread, scales).reshape(16, LANES)
                    values = [total]
                    if halves:
                        values.append(pltpu.roll(total, tail, 1))
                        if keep_right:
                            values.reverse()
                    for place, value in enumerate(values):
                        start = (group * step + place) * part + chunk * 16
                        store(tile, slice(start, start + 16), value.astype(BF16))

    def store_plain(out):
        def store(tile, rows, value):
            width = min(LANES, channels - tile * LANES)
            out[rows, tile * LANES : tile * LANES + width] = value[:, :width]

        return store

    def store_heads(which):
        def store(tile, rows, value):
            if tile * LANES < full:
                at, low, high = which * full + tile * LANES, 0, LANES
            else:
                at, low = 3 * full + which // 2 * LANES, which % 2 * tail
                high = LANES if which == 2 else low + tail
            qkv_out[rows, at + low : at + high] = value[:, low:high]

        return store

    copies[1].wait()
    for tap in range(9):
        square(conv_ref[tap], store_plain(mix_out.at[tap]))
    copies[2].wait()

    @pl.when(lax.axis_index("segment") >= first_skip)
    def _():
        square(skip_ref[...], store_plain(mix_out.at[9]))

    for copy in copies[3:10]:
        copy.wait()
    half = channels // 2
    lane = lax.broadcasted_iota(jnp.int32, (8, channels), 1)
    place = jnp.where(lane < half, lane, lane - half).astype(F32)
    frequency = jnp.exp(-math.log(10000.0) * place / half)
    for batch in range(term_out.shape[0]):
        angles = time_ref[batch].astype(F32) * frequency
        features = jnp.where(lane < half, jnp.cos(angles), jnp.sin(angles)).astype(BF16)
        term_out[batch] = dot(features, proj_ref[...])
    meta_out[0] = flag_ref[0]
    meta_out[1] = offset_ref[0]
    for copy in copies[10:]:
        copy.wait()

    @pl.when(flag_ref[0] == 1)
    def _():
        for which in range(3):
            square(attn_ref[which], store_heads(which), which == 1)
        square(attn_ref[3], store_plain(out_out))

        def widen(value):
            value = value.astype(F32)
            return value[:, :full], jnp.concatenate([value[:, full:]] * 2, axis=1)

        def wide_block(factors, out, rows, fixed, place_of):
            for place in range(QUAT):
                scales = [rule(i, *place_of(fixed, place)) for i in range(QUAT)]
                value = combine([whole for whole, _ in factors], scales)
                out[rows, place * full : (place + 1) * full] = value.astype(BF16)
            for pair in range(QUAT // 2):
                scales = []
                for i in range(QUAT):
                    left = rule(i, *place_of(fixed, 2 * pair))
                    right = rule(i, *place_of(fixed, 2 * pair + 1))
                    scales.append(jnp.where(on_left, left, right)[None])
                halves = [half.reshape(2, 8, LANES) for _, half in factors]
                value = combine(halves, scales).reshape(16, LANES)
                at = QUAT * full + pair * LANES
                out[rows, at : at + LANES] = value.astype(BF16)

        def wide_step(chunk, carry):
            start = pl.multiple_of(chunk * 16, 16)
            ups = [widen(up_ref[i, pl.ds(start, 16), :]) for i in range(QUAT)]
            downs = [widen(down_ref[i, pl.ds(start, 16), :]) for i in range(QUAT)]
            for fixed in range(QUAT):
                rows = pl.ds(pl.multiple_of(fixed * part + start, 16), 16)
                wide_block(ups, up_out, rows, fixed, lambda a, b: (a, b))
                wide_block(downs, down_out, rows, fixed, lambda b, a: (a, b))
            return carry

        lax.fori_loop(0, part // 16, wide_step, 0)


def section_weights(
    first_skip, rule, timesteps, flag, offset, scales, gains, conv, attn, up, down, skip, proj, hidden
):
    channels = proj.shape[0]
    padded = channels // LANES * LANES + LANES
    wide = up.shape[-1]
    operands = (
        rule, timesteps, flag, offset, scales, gains, conv, attn, up, down, skip, proj, hidden,
    )
    return pl.pallas_call(
        functools.partial(weights_kernel, first_skip),
        out_shape=(
            pltpu.VMEM((10, channels, channels), BF16),
            pltpu.VMEM((channels, 8 * LANES), BF16),
            pltpu.VMEM((channels, channels), BF16),
            pltpu.VMEM((channels, QUAT * wide), BF16),
            pltpu.VMEM((channels, QUAT * wide), BF16),
            pltpu.VMEM((hidden.shape[0], 8, channels), F32),
            pltpu.VMEM(gains.shape, F32),
            pltpu.SMEM((2,), jnp.int32),
            pltpu.SMEM(scales.shape, F32),
            pltpu.VMEM(hidden.shape, BF16),
        ),
        in_specs=[HBM] * len(operands),
        out_specs=(VMEM,) * 7 + (SMEM,) * 2 + (VMEM,),
        scratch_shapes=[
            pltpu.SMEM(rule.shape, F32),
            pltpu.SMEM(timesteps.shape, jnp.int32),
            pltpu.SMEM((1,), jnp.int32),
            pltpu.SMEM((1,), jnp.int32),
        ]
        + [pltpu.VMEM(array.shape, BF16) for array in (conv, attn, up, down, skip, proj)]
        + [
            pltpu.VMEM((QUAT * QUAT, 8, padded), F32),
            pltpu.VMEM((QUAT * QUAT // 2, 8, LANES), F32),
            pltpu.SemaphoreType.DMA((len(operands),)),
        ],
        compiler_params=pltpu.CompilerParams(vmem_limit_bytes=12 * MIB),
        name="weights",
    )(*[in_hbm(v) if v.size > 1 else v for v in operands])


def is_active(tick, batches):
    batch = tick - lax.axis_index("segment")
    return (batch >= 0) & (batch < batches)


def shift_columns(normed, columns):
    total = normed.shape[0]
    col = lax.rem(lax.broadcasted_iota(jnp.int32, (total, 1), 0), columns)
    left = jnp.where(col == 0, 0.0, pltpu.roll(normed, 1, 0)).astype(BF16)
    right = jnp.where(col == columns - 1, 0.0, pltpu.roll(normed, total - 1, 0)).astype(BF16)
    return [left, normed.astype(BF16), right]


def inner_kernel(columns, tick, batches, with_skip, *refs):
    if tick is None:
        tick_ref, *refs = refs
        tick = tick_ref[0]
    if with_skip:
        z_ref, *refs = refs
    x_ref, mix_ref, term_ref, gain_ref, sum_ref = refs
    tokens, channels = x_ref.shape

    @pl.when(is_active(tick, batches))
    def _():
        shifted = shift_columns(rms(x_ref[...].astype(F32), gain_ref[0]), columns)
        edge = jnp.zeros((columns, channels), BF16)
        hidden = jnp.broadcast_to(term_ref[0:1, :], (tokens, channels))
        if with_skip:
            hidden = hidden + dot(z_ref[...], mix_ref[9])
        for b in range(3):
            hidden = hidden + dot(shifted[b], mix_ref[3 + b])
        for b in range(3):
            rows = jnp.concatenate([edge, shifted[b][: tokens - columns]], axis=0)
            hidden = hidden + dot(rows, mix_ref[b])
        for b in range(3):
            rows = jnp.concatenate([shifted[b][columns:], edge], axis=0)
            hidden = hidden + dot(rows, mix_ref[6 + b])
        sum_ref[...] = hidden


def attention(normed, qkv_ref, scales_ref, offset, columns):
    tokens = normed.shape[0]
    projected = dot(normed, qkv_ref[...]).astype(BF16)
    tiles = [projected[:, t * LANES : (t + 1) * LANES] for t in range(8)]
    lane = lax.broadcasted_iota(jnp.int32, (tokens, LANES), 1)
    left = lane < HEAD

    groups = lax.broadcasted_iota(jnp.int32, (LANES, LANES), 0) // HEAD
    groups = groups == lax.broadcasted_iota(jnp.int32, (LANES, LANES), 1) // HEAD
    groups = jnp.where(groups, 1.0, 0.0).astype(BF16)
    scaled = [tiles[t].astype(F32) for t in (0, 1, 2, 3, 6)]
    squares = jnp.concatenate([(v * v).astype(BF16) for v in scaled], axis=0)
    inverse = lax.rsqrt(dot(squares, groups) + COS_EPSILON)
    factors = [
        jnp.where(left, scales_ref[0, 0], scales_ref[0, 1]),
        jnp.where(left, scales_ref[0, 2], scales_ref[0, 3]),
        None,
        None,
        jnp.where(left, scales_ref[0, 4], 1.0),
    ]
    units = []
    for place, (value, factor) in enumerate(zip(scaled, factors)):
        norm = inverse[place * tokens : (place + 1) * tokens]
        units.append(value * (norm if factor is None else norm * factor))
    last_key = pltpu.roll(units[4], HEAD, 1).astype(BF16)
    units = [value.astype(BF16) for value in units]

    def window(index):
        return lax.rem(lax.rem(index, columns) - offset + columns, columns) // WIN

    row_window = window(lax.broadcasted_iota(jnp.int32, (tokens, 1), 0))
    same = row_window == window(lax.broadcasted_iota(jnp.int32, (1, tokens), 1))
    zero, one = jnp.zeros((), BF16), jnp.ones((), BF16)

    def weights(query, keys):
        return jnp.where(same, jnp.exp(dot_t(query, keys)), 0.0).astype(BF16)

    mixed = []
    for t in range(2):
        even = weights(jnp.where(left, units[t], zero), units[2 + t])
        odd = weights(jnp.where(left, zero, units[t]), units[2 + t])
        even = dot(even, jnp.where(left, tiles[4 + t], one))
        odd = dot(odd, jnp.where(left, one, tiles[4 + t]))
        sums = pltpu.roll(jnp.where(left, odd, even), HEAD, 1)
        mixed.append((jnp.where(left, even, odd) / sums).astype(BF16))
    even = weights(jnp.where(left, units[4], zero), last_key)
    even = dot(even, jnp.where(left, tiles[7], one))
    mixed.append((even / pltpu.roll(even, HEAD, 1)).astype(BF16)[:, :HEAD])
    return jnp.concatenate(mixed, axis=1)


def outer_kernel(columns, tick, batches, *refs):
    if tick is None:
        tick_ref, *refs = refs
        tick = tick_ref[0]
    (
        meta_ref, scales_ref, x_ref, sum_ref, low_ref, high_ref, prev_ref, mix_ref, qkv_ref,
        proj_ref, up_ref, down_ref, gain_ref, out_ref, first_ref, last_ref,
    ) = refs
    tokens, channels = x_ref.shape
    active = is_active(tick, batches)

    def write(x3):
        value = x3.astype(BF16)
        out_ref[...] = value
        first_ref[...] = value[:columns]
        last_ref[...] = value[tokens - columns :]

    @pl.when(jnp.logical_not(active))
    def _():
        out_ref[...] = prev_ref[...]

    @pl.when(active)
    def _():
        gain = [gain_ref[row] for row in range(3)]
        below = low_ref.shape[0] - columns
        low = shift_columns(rms(low_ref[below:].astype(F32), gain[0]), columns)
        high = shift_columns(rms(high_ref[:columns].astype(F32), gain[0]), columns)
        top = sum_ref[:columns]
        bottom = sum_ref[tokens - columns :]
        for b in range(3):
            top = top + dot(low[b], mix_ref[b])
            bottom = bottom + dot(high[b], mix_ref[6 + b])
        hidden = jnp.concatenate([top, sum_ref[columns : tokens - columns], bottom], axis=0)
        x1 = x_ref[...].astype(F32) + silu(hidden)
        has_block, offset = meta_ref[0], meta_ref[1]

        @pl.when(has_block != 1)
        def _():
            write(x1)

        @pl.when(has_block == 1)
        def _():
            n2 = rms(x1, gain[1]).astype(BF16)
            heads = attention(n2, qkv_ref, scales_ref, offset, columns)
            x2 = x1 + dot(heads, proj_ref[...])
            n3 = rms(x2, gain[2]).astype(BF16)
            act = silu(dot(n3, up_ref[...])).astype(BF16)
            x3 = x2 + dot_t(act, down_ref[...])
            write(x3)


def run_inner(columns, tick, batches, x, z, mix, term, gains):
    static = isinstance(tick, int)
    with_skip = z is not None
    operands = [z] if with_skip else []
    operands += [x, in_vmem(mix), term, in_vmem(gains)]
    specs = [VMEM] * len(operands)
    if not static:
        operands, specs = [tick] + operands, [SMEM] + specs
    return pl.pallas_call(
        functools.partial(inner_kernel, columns, tick if static else None, batches, with_skip),
        out_shape=pltpu.VMEM(x.shape, F32),
        in_specs=specs,
        out_specs=VMEM,
        compiler_params=pltpu.CompilerParams(vmem_limit_bytes=8 * MIB),
        name="inner",
    )(*operands)


def run_outer(columns, tick, batches, x, total, low, high, prev, weights):
    static = isinstance(tick, int)
    mix, qkv, proj, up, down, gains, meta, scales = weights
    operands = [in_smem(meta), in_smem(scales), x, in_vmem(total), low, high, prev]
    operands += [in_vmem(w) for w in (mix, qkv, proj, up, down, gains)]
    specs = [SMEM] * 2 + [VMEM] * (len(operands) - 2)
    if not static:
        operands, specs = [tick] + operands, [SMEM] + specs
    edge = jax.ShapeDtypeStruct((columns, x.shape[1]), BF16)
    return pl.pallas_call(
        functools.partial(outer_kernel, columns, tick if static else None, batches),
        out_shape=(jax.ShapeDtypeStruct(x.shape, BF16), edge, edge),
        in_specs=specs,
        out_specs=(VMEM,) * 3,
        compiler_params=pltpu.CompilerParams(vmem_limit_bytes=8 * MIB),
        name="outer",
    )(*operands)


def shards(
    hidden, timesteps, rule_matrices, conv_factors, time_proj, skip_factors, attn_factors,
    up_factors, down_factors, norm_gains, head_scales, has_block, offsets,
):
    segments = lax.axis_size("segment")
    row_parts = lax.axis_size("rows")
    half = segments // 2
    segment = lax.axis_index("segment")
    batches, height, columns, channels = hidden.shape
    tokens = height * columns
    axes = ("segment", "rows")

    def pairs(sources, step, turn):
        return [
            (s * row_parts + r, (s + step) * row_parts + r + turn)
            for s in sources
            for r in range(row_parts)
            if 0 <= s + step < segments and 0 <= r + turn < row_parts
        ]

    def pass_on(value, sources, step, turn):
        links = pairs(sources, step, turn)
        if not links:
            return jnp.zeros_like(value)
        return lax.ppermute(value, axes, links)

    flat = hidden.reshape(batches, tokens, channels)
    near, far = min(1, segments - 1), min(2, segments - 1)
    low0 = pass_on(flat, [near], -near, 1)
    high0 = pass_on(flat, [far], -far, -1)
    mix, qkv, proj, up, down, terms, gains, meta, scales, flat = section_weights(
        half if batches == 1 else 0,
        rule_matrices[0], timesteps, has_block, offsets, head_scales,
        jnp.transpose(norm_gains, (1, 0, 2)), conv_factors[0], attn_factors[0], up_factors[0],
        jnp.transpose(down_factors[0], (0, 2, 1)), skip_factors[0], time_proj[0], flat,
    )
    weights = (mix, qkv, proj, up, down, gains, meta, scales)

    def section(tick, x, low, high, z, prev, term):
        total = run_inner(columns, tick, batches, x, z, mix, term, gains)
        return run_outer(columns, tick, batches, x, total, low, high, prev, weights)

    def edges_on(out, first, last, sources):
        main = pass_on(out, sources, 1, 0)
        low = pass_on(last, sources, 1, 1)
        high = pass_on(first, sources, 1, -1)
        return main, low, high

    if batches == 1:
        x, low, high = flat[0], low0[0], high0[0]
        out = flat[0]
        skips = []
        for tick in range(segments):
            z = skips[tick - half] if tick >= half else None
            out, first, last = section(tick, x, low, high, z, out, terms[0])
            if tick + 1 < segments:
                x, low, high = edges_on(out, first, last, [tick])
                skips.append(pass_on(out, [tick], half, 0) if tick + half < segments else None)
        return out.reshape(1, batches, height, columns, channels)

    def pick(array, slot):
        return lax.dynamic_index_in_dim(array, slot, 0, keepdims=False)

    def tick_step(tick, state):
        states, received, skip_buffer = state
        slot = jnp.clip(tick - segment, 0, batches - 1)
        own = pick(flat, slot), pick(low0, slot)[tokens - columns :], pick(high0, slot)[:columns]
        x, low, high = [jnp.where(segment == 0, f, r) for f, r in zip(own, received)]
        out, first, last = section(
            jnp.reshape(tick, (1,)), x, low, high, pick(skip_buffer, slot), pick(states, slot),
            pick(terms, slot),
        )
        states = lax.dynamic_update_index_in_dim(states, out, slot, 0)
        passed = edges_on(out, first, last, range(segments))
        arrived = pass_on(out, range(segments), half, 0)
        partner = tick - segment + half
        fits = (segment >= half) & (partner >= 0) & (partner < batches)
        partner_slot = jnp.clip(partner, 0, batches - 1)
        kept = pick(skip_buffer, partner_slot)
        skip_buffer = lax.dynamic_update_index_in_dim(
            skip_buffer, jnp.where(fits, arrived, kept), partner_slot, 0
        )
        return states, passed, skip_buffer

    edge = jnp.zeros((columns, channels), BF16)
    initial = (jnp.zeros_like(flat), (jnp.zeros_like(flat[0]), edge, edge), jnp.zeros_like(flat))
    states = lax.fori_loop(0, batches + segments - 1, tick_step, initial)[0]
    return states.reshape(1, batches, height, columns, channels)


def solution(mesh):
    return jax.shard_map(
        shards,
        mesh=mesh,
        in_specs=(
            P("groups", "rows", None, None),
            P("groups"),
            P("segment", None, None, None),
            P("segment", None, None, None, None),
            P("segment", None, None),
            P("segment", None, None, None),
            P("segment", None, None, None, None),
            P("segment", None, None, None),
            P("segment", None, None, None),
            P("segment", None, None),
            P("segment", None),
            P("segment"),
            P("segment"),
        ),
        out_specs=P("segment", "groups", "rows", None, None),
        check_vma=False,
    )
```

```python
import functools
import math

import jax
import jax.numpy as jnp
from jax import lax
from jax.experimental import pallas as pl
from jax.experimental.pallas import tpu as pltpu
from jax.sharding import PartitionSpec as P

HEAD = 64
WIN = 8
QUAT = 4

EPSILON = 1e-05
COS_EPSILON = 1e-06

F32 = jnp.float32
BF16 = jnp.bfloat16
MIB = 1024 * 1024
LANES = 128

VMEM = pl.BlockSpec(memory_space=pltpu.VMEM)
SMEM = pl.BlockSpec(memory_space=pltpu.SMEM)
HBM = pl.BlockSpec(memory_space=pltpu.HBM)


def in_vmem(value):
    return pltpu.with_memory_space_constraint(value, pltpu.VMEM)


def in_smem(value):
    return pltpu.with_memory_space_constraint(value, pltpu.SMEM)


def in_hbm(value):
    return pltpu.with_memory_space_constraint(value, pltpu.HBM)


def dot(left, right):
    return jnp.dot(left, right, preferred_element_type=F32)


def dot_t(left, right):
    return lax.dot_general(left, right, (((1,), (1,)), ((), ())), preferred_element_type=F32)


def rms(values, gain_row):
    mean_square = jnp.mean(values * values, axis=-1, keepdims=True)
    return values * lax.rsqrt(mean_square + EPSILON) * gain_row


def silu(values):
    return values / (1.0 + jnp.exp(-values))


def weights_kernel(
    first_skip, rule_hbm, time_hbm, flag_hbm, offset_hbm, scale_hbm, gain_hbm,
    conv_hbm, attn_hbm, up_hbm, down_hbm, skip_hbm, proj_hbm, hidden_hbm,
    mix_out, qkv_out, out_out, up_out, down_out, term_out, gain_out, meta_out, scale_out,
    hidden_out,
    rule_ref, time_ref, flag_ref, offset_ref, conv_ref, attn_ref, up_ref, down_ref,
    skip_ref, proj_ref, rows_ref, pair_ref, sems,
):
    sources = [
        rule_hbm, conv_hbm, skip_hbm, time_hbm, proj_hbm, flag_hbm, offset_hbm, scale_hbm,
        gain_hbm, hidden_hbm, attn_hbm, up_hbm, down_hbm,
    ]
    targets = [
        rule_ref, conv_ref, skip_ref, time_ref, proj_ref, flag_ref, offset_ref, scale_out,
        gain_out, hidden_out, attn_ref, up_ref, down_ref,
    ]
    copies = [
        pltpu.make_async_copy(source, target, sems.at[place])
        for place, (source, target) in enumerate(zip(sources, targets))
    ]
    for copy in copies:
        copy.start()
    part = conv_ref.shape[-1]

    def rule(i, a, b):
        return rule_ref[i, a, b]

    channels = proj_ref.shape[0]
    tail = channels % LANES
    full = channels - tail
    padded = full + LANES

    def channel_of(lane):
        return jnp.where(lane < channels, lane, lane - tail)

    lanes = channel_of(lax.broadcasted_iota(jnp.int32, (part, padded), 1))
    ones = lax.rem(lanes, part) == lax.broadcasted_iota(jnp.int32, (part, padded), 0)
    repeat = jnp.where(ones, 1.0, 0.0).astype(BF16)
    copies[0].wait()
    block = channel_of(lax.broadcasted_iota(jnp.int32, (8, padded), 1)) // part
    for i in range(QUAT):
        for a in range(QUAT):
            row = jnp.where(block == 0, rule(i, a, 0), rule(i, a, 1))
            row = jnp.where(block == 2, rule(i, a, 2), row)
            rows_ref[i * QUAT + a] = jnp.where(block == 3, rule(i, a, 3), row)
    on_left = lax.broadcasted_iota(jnp.int32, (8, LANES), 1) < tail
    for place in range(QUAT * QUAT // 2):
        left, right = rows_ref[2 * place, :, full:], rows_ref[2 * place + 1, :, full:]
        pair_ref[place] = jnp.where(on_left, left, right)

    def combine(parts, scales):
        total = parts[0] * scales[0]
        for value, scale in zip(parts[1:], scales[1:]):
            total = total + value * scale
        return total

    def square(factors, store, keep_right=False):
        stacked = factors.reshape(QUAT * part, part)
        for tile in range(padded // LANES):
            at = slice(tile * LANES, (tile + 1) * LANES)
            halves = tile * LANES == full
            if halves:
                rows = [pair_ref[place][None] for place in range(QUAT * QUAT // 2)]
            else:
                rows = [rows_ref[place, :, at][None] for place in range(QUAT * QUAT)]
            step = 2 if halves else 1
            groups = QUAT // step
            whole = dot(stacked, repeat[:, at])
            for chunk in range(part // 16):
                spread = [
                    whole[i * part + chunk * 16 : i * part + (chunk + 1) * 16]
                    for i in range(QUAT)
                ]
                spread = [value.reshape(2, 8, LANES) for value in spread]
                for group in range(groups):
                    scales = [rows[i * groups + group] for i in range(QUAT)]
                    total = combine(spread, scales).reshape(16, LANES)
                    values = [total]
                    if halves:
                        values.append(pltpu.roll(total, tail, 1))
                        if keep_right:
                            values.reverse()
                    for place, value in enumerate(values):
                        start = (group * step + place) * part + chunk * 16
                        store(tile, slice(start, start + 16), value.astype(BF16))

    def store_plain(out):
        def store(tile, rows, value):
            width = min(LANES, channels - tile * LANES)
            out[rows, tile * LANES : tile * LANES + width] = value[:, :width]

        return store

    def store_heads(which):
        def store(tile, rows, value):
            if tile * LANES < full:
                at, low, high = which * full + tile * LANES, 0, LANES
            else:
                at, low = 3 * full + which // 2 * LANES, which % 2 * tail
                high = LANES if which == 2 else low + tail
            qkv_out[rows, at + low : at + high] = value[:, low:high]

        return store

    copies[1].wait()
    for tap in range(9):
        square(conv_ref[tap], store_plain(mix_out.at[tap]))
    copies[2].wait()

    @pl.when(lax.axis_index("segment") >= first_skip)
    def _():
        square(skip_ref[...], store_plain(mix_out.at[9]))

    for copy in copies[3:10]:
        copy.wait()
    half = channels // 2
    lane = lax.broadcasted_iota(jnp.int32, (8, channels), 1)
    place = jnp.where(lane < half, lane, lane - half).astype(F32)
    frequency = jnp.exp(-math.log(10000.0) * place / half)
    for batch in range(term_out.shape[0]):
        angles = time_ref[batch].astype(F32) * frequency
        features = jnp.where(lane < half, jnp.cos(angles), jnp.sin(angles)).astype(BF16)
        term_out[batch] = dot(features, proj_ref[...])
    meta_out[0] = flag_ref[0]
    meta_out[1] = offset_ref[0]
    for copy in copies[10:]:
        copy.wait()

    @pl.when(flag_ref[0] == 1)
    def _():
        for which in range(3):
            square(attn_ref[which], store_heads(which), which == 1)
        square(attn_ref[3], store_plain(out_out))

        def widen(value):
            value = value.astype(F32)
            return value[:, :full], jnp.concatenate([value[:, full:]] * 2, axis=1)

        def wide_block(factors, out, rows, fixed, place_of):
            for place in range(QUAT):
                scales = [rule(i, *place_of(fixed, place)) for i in range(QUAT)]
                value = combine([whole for whole, _ in factors], scales)
                out[rows, place * full : (place + 1) * full] = value.astype(BF16)
            for pair in range(QUAT // 2):
                scales = []
                for i in range(QUAT):
                    left = rule(i, *place_of(fixed, 2 * pair))
                    right = rule(i, *place_of(fixed, 2 * pair + 1))
                    scales.append(jnp.where(on_left, left, right)[None])
                halves = [half.reshape(2, 8, LANES) for _, half in factors]
                value = combine(halves, scales).reshape(16, LANES)
                at = QUAT * full + pair * LANES
                out[rows, at : at + LANES] = value.astype(BF16)

        def wide_step(chunk, carry):
            start = pl.multiple_of(chunk * 16, 16)
            ups = [widen(up_ref[i, pl.ds(start, 16), :]) for i in range(QUAT)]
            downs = [widen(down_ref[i, pl.ds(start, 16), :]) for i in range(QUAT)]
            for fixed in range(QUAT):
                rows = pl.ds(pl.multiple_of(fixed * part + start, 16), 16)
                wide_block(ups, up_out, rows, fixed, lambda a, b: (a, b))
                wide_block(downs, down_out, rows, fixed, lambda b, a: (a, b))
            return carry

        lax.fori_loop(0, part // 16, wide_step, 0, unroll=True)


def section_weights(
    first_skip, rule, timesteps, flag, offset, scales, gains, conv, attn, up, down, skip, proj, hidden
):
    channels = proj.shape[0]
    padded = channels // LANES * LANES + LANES
    wide = up.shape[-1]
    operands = (
        rule, timesteps, flag, offset, scales, gains, conv, attn, up, down, skip, proj, hidden,
    )
    return pl.pallas_call(
        functools.partial(weights_kernel, first_skip),
        out_shape=(
            pltpu.VMEM((10, channels, channels), BF16),
            pltpu.VMEM((channels, 8 * LANES), BF16),
            pltpu.VMEM((channels, channels), BF16),
            pltpu.VMEM((channels, QUAT * wide), BF16),
            pltpu.VMEM((channels, QUAT * wide), BF16),
            pltpu.VMEM((hidden.shape[0], 8, channels), F32),
            pltpu.VMEM(gains.shape, F32),
            pltpu.SMEM((2,), jnp.int32),
            pltpu.SMEM(scales.shape, F32),
            pltpu.VMEM(hidden.shape, BF16),
        ),
        in_specs=[HBM] * len(operands),
        out_specs=(VMEM,) * 7 + (SMEM,) * 2 + (VMEM,),
        scratch_shapes=[
            pltpu.SMEM(rule.shape, F32),
            pltpu.SMEM(timesteps.shape, jnp.int32),
            pltpu.SMEM((1,), jnp.int32),
            pltpu.SMEM((1,), jnp.int32),
        ]
        + [pltpu.VMEM(array.shape, BF16) for array in (conv, attn, up, down, skip, proj)]
        + [
            pltpu.VMEM((QUAT * QUAT, 8, padded), F32),
            pltpu.VMEM((QUAT * QUAT // 2, 8, LANES), F32),
            pltpu.SemaphoreType.DMA((len(operands),)),
        ],
        compiler_params=pltpu.CompilerParams(vmem_limit_bytes=12 * MIB),
        name="weights",
    )(*[in_hbm(v) if v.size > 1 else v for v in operands])


def is_active(tick, batches):
    batch = tick - lax.axis_index("segment")
    return (batch >= 0) & (batch < batches)


def shift_columns(normed, columns):
    total = normed.shape[0]
    col = lax.rem(lax.broadcasted_iota(jnp.int32, (total, 1), 0), columns)
    left = jnp.where(col == 0, 0.0, pltpu.roll(normed, 1, 0)).astype(BF16)
    right = jnp.where(col == columns - 1, 0.0, pltpu.roll(normed, total - 1, 0)).astype(BF16)
    return [left, normed.astype(BF16), right]


def inner_kernel(columns, tick, batches, with_skip, *refs):
    if tick is None:
        tick_ref, *refs = refs
        tick = tick_ref[0]
    if with_skip:
        z_ref, *refs = refs
    x_ref, mix_ref, term_ref, gain_ref, sum_ref = refs
    tokens, channels = x_ref.shape

    @pl.when(is_active(tick, batches))
    def _():
        shifted = shift_columns(rms(x_ref[...].astype(F32), gain_ref[0]), columns)
        edge = jnp.zeros((columns, channels), BF16)
        hidden = jnp.broadcast_to(term_ref[0:1, :], (tokens, channels))
        if with_skip:
            hidden = hidden + dot(z_ref[...], mix_ref[9])
        for b in range(3):
            hidden = hidden + dot(shifted[b], mix_ref[3 + b])
        for b in range(3):
            rows = jnp.concatenate([edge, shifted[b][: tokens - columns]], axis=0)
            hidden = hidden + dot(rows, mix_ref[b])
        for b in range(3):
            rows = jnp.concatenate([shifted[b][columns:], edge], axis=0)
            hidden = hidden + dot(rows, mix_ref[6 + b])
        sum_ref[...] = hidden


def attention(normed, qkv_ref, scales_ref, offset, columns):
    tokens = normed.shape[0]
    projected = dot(normed, qkv_ref[...]).astype(BF16)
    tiles = [projected[:, t * LANES : (t + 1) * LANES] for t in range(8)]
    lane = lax.broadcasted_iota(jnp.int32, (tokens, LANES), 1)
    left = lane < HEAD

    groups = lax.broadcasted_iota(jnp.int32, (LANES, LANES), 0) // HEAD
    groups = groups == lax.broadcasted_iota(jnp.int32, (LANES, LANES), 1) // HEAD
    groups = jnp.where(groups, 1.0, 0.0).astype(BF16)
    scaled = [tiles[t].astype(F32) for t in (0, 1, 2, 3, 6)]
    squares = jnp.concatenate([(v * v).astype(BF16) for v in scaled], axis=0)
    inverse = lax.rsqrt(dot(squares, groups) + COS_EPSILON)
    factors = [
        jnp.where(left, scales_ref[0, 0], scales_ref[0, 1]),
        jnp.where(left, scales_ref[0, 2], scales_ref[0, 3]),
        None,
        None,
        jnp.where(left, scales_ref[0, 4], 1.0),
    ]
    units = []
    for place, (value, factor) in enumerate(zip(scaled, factors)):
        norm = inverse[place * tokens : (place + 1) * tokens]
        units.append(value * (norm if factor is None else norm * factor))
    last_key = pltpu.roll(units[4], HEAD, 1).astype(BF16)
    units = [value.astype(BF16) for value in units]

    def window(index):
        return lax.rem(lax.rem(index, columns) - offset + columns, columns) // WIN

    row_window = window(lax.broadcasted_iota(jnp.int32, (tokens, 1), 0))
    same = row_window == window(lax.broadcasted_iota(jnp.int32, (1, tokens), 1))
    zero, one = jnp.zeros((), BF16), jnp.ones((), BF16)

    def weights(query, keys):
        return jnp.where(same, jnp.exp(dot_t(query, keys)), 0.0).astype(BF16)

    mixed = []
    for t in range(2):
        even = weights(jnp.where(left, units[t], zero), units[2 + t])
        odd = weights(jnp.where(left, zero, units[t]), units[2 + t])
        even = dot(even, jnp.where(left, tiles[4 + t], one))
        odd = dot(odd, jnp.where(left, one, tiles[4 + t]))
        sums = pltpu.roll(jnp.where(left, odd, even), HEAD, 1)
        mixed.append((jnp.where(left, even, odd) / sums).astype(BF16))
    even = weights(jnp.where(left, units[4], zero), last_key)
    even = dot(even, jnp.where(left, tiles[7], one))
    mixed.append((even / pltpu.roll(even, HEAD, 1)).astype(BF16)[:, :HEAD])
    return jnp.concatenate(mixed, axis=1)


def outer_kernel(columns, tick, batches, *refs):
    if tick is None:
        tick_ref, *refs = refs
        tick = tick_ref[0]
    (
        meta_ref, scales_ref, x_ref, sum_ref, low_ref, high_ref, prev_ref, mix_ref, qkv_ref,
        proj_ref, up_ref, down_ref, gain_ref, out_ref, first_ref, last_ref,
    ) = refs
    tokens, channels = x_ref.shape
    active = is_active(tick, batches)

    def write(x3):
        value = x3.astype(BF16)
        out_ref[...] = value
        first_ref[...] = value[:columns]
        last_ref[...] = value[tokens - columns :]

    @pl.when(jnp.logical_not(active))
    def _():
        out_ref[...] = prev_ref[...]

    @pl.when(active)
    def _():
        gain = [gain_ref[row] for row in range(3)]
        below = low_ref.shape[0] - columns
        low = shift_columns(rms(low_ref[below:].astype(F32), gain[0]), columns)
        high = shift_columns(rms(high_ref[:columns].astype(F32), gain[0]), columns)
        top = sum_ref[:columns]
        bottom = sum_ref[tokens - columns :]
        for b in range(3):
            top = top + dot(low[b], mix_ref[b])
            bottom = bottom + dot(high[b], mix_ref[6 + b])
        hidden = jnp.concatenate([top, sum_ref[columns : tokens - columns], bottom], axis=0)
        x1 = x_ref[...].astype(F32) + silu(hidden)
        has_block, offset = meta_ref[0], meta_ref[1]

        @pl.when(has_block != 1)
        def _():
            write(x1)

        @pl.when(has_block == 1)
        def _():
            n2 = rms(x1, gain[1]).astype(BF16)
            heads = attention(n2, qkv_ref, scales_ref, offset, columns)
            x2 = x1 + dot(heads, proj_ref[...])
            n3 = rms(x2, gain[2]).astype(BF16)
            act = silu(dot(n3, up_ref[...])).astype(BF16)
            x3 = x2 + dot_t(act, down_ref[...])
            write(x3)


def run_inner(columns, tick, batches, x, z, mix, term, gains):
    static = isinstance(tick, int)
    with_skip = z is not None
    operands = [z] if with_skip else []
    operands += [x, in_vmem(mix), term, in_vmem(gains)]
    specs = [VMEM] * len(operands)
    if not static:
        operands, specs = [tick] + operands, [SMEM] + specs
    return pl.pallas_call(
        functools.partial(inner_kernel, columns, tick if static else None, batches, with_skip),
        out_shape=pltpu.VMEM(x.shape, F32),
        in_specs=specs,
        out_specs=VMEM,
        compiler_params=pltpu.CompilerParams(vmem_limit_bytes=8 * MIB),
        name="inner",
    )(*operands)


def run_outer(columns, tick, batches, x, total, low, high, prev, weights):
    static = isinstance(tick, int)
    mix, qkv, proj, up, down, gains, meta, scales = weights
    operands = [in_smem(meta), in_smem(scales), x, in_vmem(total), low, high, prev]
    operands += [in_vmem(w) for w in (mix, qkv, proj, up, down, gains)]
    specs = [SMEM] * 2 + [VMEM] * (len(operands) - 2)
    if not static:
        operands, specs = [tick] + operands, [SMEM] + specs
    edge = jax.ShapeDtypeStruct((columns, x.shape[1]), BF16)
    return pl.pallas_call(
        functools.partial(outer_kernel, columns, tick if static else None, batches),
        out_shape=(jax.ShapeDtypeStruct(x.shape, BF16), edge, edge),
        in_specs=specs,
        out_specs=(VMEM,) * 3,
        compiler_params=pltpu.CompilerParams(vmem_limit_bytes=8 * MIB),
        name="outer",
    )(*operands)


def shards(
    hidden, timesteps, rule_matrices, conv_factors, time_proj, skip_factors, attn_factors,
    up_factors, down_factors, norm_gains, head_scales, has_block, offsets,
):
    segments = lax.axis_size("segment")
    row_parts = lax.axis_size("rows")
    half = segments // 2
    segment = lax.axis_index("segment")
    batches, height, columns, channels = hidden.shape
    tokens = height * columns
    axes = ("segment", "rows")

    def pairs(sources, step, turn):
        return [
            (s * row_parts + r, (s + step) * row_parts + r + turn)
            for s in sources
            for r in range(row_parts)
            if 0 <= s + step < segments and 0 <= r + turn < row_parts
        ]

    def pass_on(value, sources, step, turn):
        links = pairs(sources, step, turn)
        if not links:
            return jnp.zeros_like(value)
        return lax.ppermute(value, axes, links)

    flat = hidden.reshape(batches, tokens, channels)
    near, far = min(1, segments - 1), min(2, segments - 1)
    low0 = pass_on(flat, [near], -near, 1)
    high0 = pass_on(flat, [far], -far, -1)
    mix, qkv, proj, up, down, terms, gains, meta, scales, flat = section_weights(
        half if batches == 1 else 0,
        rule_matrices[0], timesteps, has_block, offsets, head_scales,
        jnp.transpose(norm_gains, (1, 0, 2)), conv_factors[0], attn_factors[0], up_factors[0],
        jnp.transpose(down_factors[0], (0, 2, 1)), skip_factors[0], time_proj[0], flat,
    )
    weights = (mix, qkv, proj, up, down, gains, meta, scales)

    def section(tick, x, low, high, z, prev, term):
        total = run_inner(columns, tick, batches, x, z, mix, term, gains)
        return run_outer(columns, tick, batches, x, total, low, high, prev, weights)

    def edges_on(out, first, last, sources):
        main = pass_on(out, sources, 1, 0)
        low = pass_on(last, sources, 1, 1)
        high = pass_on(first, sources, 1, -1)
        return main, low, high

    if batches == 1:
        x, low, high = flat[0], low0[0], high0[0]
        out = flat[0]
        skips = []
        for tick in range(segments):
            z = skips[tick - half] if tick >= half else None
            out, first, last = section(tick, x, low, high, z, out, terms[0])
            if tick + 1 < segments:
                x, low, high = edges_on(out, first, last, [tick])
                skips.append(pass_on(out, [tick], half, 0) if tick + half < segments else None)
        return out.reshape(1, batches, height, columns, channels)

    def pick(array, slot):
        return lax.dynamic_index_in_dim(array, slot, 0, keepdims=False)

    def tick_step(tick, state):
        states, received, skip_buffer = state
        slot = jnp.clip(tick - segment, 0, batches - 1)
        own = pick(flat, slot), pick(low0, slot)[tokens - columns :], pick(high0, slot)[:columns]
        x, low, high = [jnp.where(segment == 0, f, r) for f, r in zip(own, received)]
        out, first, last = section(
            jnp.reshape(tick, (1,)), x, low, high, pick(skip_buffer, slot), pick(states, slot),
            pick(terms, slot),
        )
        states = lax.dynamic_update_index_in_dim(states, out, slot, 0)
        passed = edges_on(out, first, last, range(segments))
        arrived = pass_on(out, range(segments), half, 0)
        partner = tick - segment + half
        fits = (segment >= half) & (partner >= 0) & (partner < batches)
        partner_slot = jnp.clip(partner, 0, batches - 1)
        kept = pick(skip_buffer, partner_slot)
        skip_buffer = lax.dynamic_update_index_in_dim(
            skip_buffer, jnp.where(fits, arrived, kept), partner_slot, 0
        )
        return states, passed, skip_buffer

    edge = jnp.zeros((columns, channels), BF16)
    initial = (jnp.zeros_like(flat), (jnp.zeros_like(flat[0]), edge, edge), jnp.zeros_like(flat))
    states = lax.fori_loop(0, batches + segments - 1, tick_step, initial)[0]
    return states.reshape(1, batches, height, columns, channels)


def solution(mesh):
    return jax.shard_map(
        shards,
        mesh=mesh,
        in_specs=(
            P("groups", "rows", None, None),
            P("groups"),
            P("segment", None, None, None),
            P("segment", None, None, None, None),
            P("segment", None, None),
            P("segment", None, None, None),
            P("segment", None, None, None, None),
            P("segment", None, None, None),
            P("segment", None, None, None),
            P("segment", None, None),
            P("segment", None),
            P("segment"),
            P("segment"),
        ),
        out_specs=P("segment", "groups", "rows", None, None),
        check_vma=False,
    )
```

```python
import functools
import math

import jax
import jax.numpy as jnp
from jax import lax
from jax.experimental import pallas as pl
from jax.experimental.pallas import tpu as pltpu
from jax.sharding import PartitionSpec as P

HEAD = 64
WIN = 8
QUAT = 4

EPSILON = 1e-05
COS_EPSILON = 1e-06

F32 = jnp.float32
BF16 = jnp.bfloat16
MIB = 1024 * 1024
LANES = 128

VMEM = pl.BlockSpec(memory_space=pltpu.VMEM)
SMEM = pl.BlockSpec(memory_space=pltpu.SMEM)
HBM = pl.BlockSpec(memory_space=pltpu.HBM)


def in_vmem(value):
    return pltpu.with_memory_space_constraint(value, pltpu.VMEM)


def in_smem(value):
    return pltpu.with_memory_space_constraint(value, pltpu.SMEM)


def in_hbm(value):
    return pltpu.with_memory_space_constraint(value, pltpu.HBM)


def dot(left, right):
    return jnp.dot(left, right, preferred_element_type=F32)


def dot_t(left, right):
    return lax.dot_general(left, right, (((1,), (1,)), ((), ())), preferred_element_type=F32)


def rms(values, gain_row):
    mean_square = jnp.mean(values * values, axis=-1, keepdims=True)
    return values * lax.rsqrt(mean_square + EPSILON) * gain_row


def silu(values):
    return values / (1.0 + jnp.exp(-values))


def weights_kernel(
    first_skip, rule_hbm, time_hbm, flag_hbm, offset_hbm, scale_hbm, gain_hbm,
    conv_hbm, attn_hbm, up_hbm, down_hbm, skip_hbm, proj_hbm, hidden_hbm,
    mix_out, qkv_out, out_out, up_out, down_out, term_out, gain_out, meta_out, scale_out,
    hidden_out,
    rule_ref, time_ref, flag_ref, offset_ref, conv_ref, attn_ref, up_ref, down_ref,
    skip_ref, proj_ref, rows_ref, pair_ref, sems,
):
    sources = [
        rule_hbm, conv_hbm, skip_hbm, time_hbm, proj_hbm, flag_hbm, offset_hbm, scale_hbm,
        gain_hbm, hidden_hbm, attn_hbm, up_hbm, down_hbm,
    ]
    targets = [
        rule_ref, conv_ref, skip_ref, time_ref, proj_ref, flag_ref, offset_ref, scale_out,
        gain_out, hidden_out, attn_ref, up_ref, down_ref,
    ]
    copies = [
        pltpu.make_async_copy(source, target, sems.at[place])
        for place, (source, target) in enumerate(zip(sources, targets))
    ]
    for place in (1, 0, *range(2, len(copies))):
        copies[place].start()
    part = conv_ref.shape[-1]

    def rule(i, a, b):
        return rule_ref[i, a, b]

    channels = proj_ref.shape[0]
    tail = channels % LANES
    full = channels - tail
    padded = full + LANES

    def channel_of(lane):
        return jnp.where(lane < channels, lane, lane - tail)

    lanes = channel_of(lax.broadcasted_iota(jnp.int32, (part, padded), 1))
    ones = lax.rem(lanes, part) == lax.broadcasted_iota(jnp.int32, (part, padded), 0)
    repeat = jnp.where(ones, 1.0, 0.0).astype(BF16)
    copies[0].wait()
    block = channel_of(lax.broadcasted_iota(jnp.int32, (8, padded), 1)) // part
    for i in range(QUAT):
        for a in range(QUAT):
            row = jnp.where(block == 0, rule(i, a, 0), rule(i, a, 1))
            row = jnp.where(block == 2, rule(i, a, 2), row)
            rows_ref[i * QUAT + a] = jnp.where(block == 3, rule(i, a, 3), row)
    on_left = lax.broadcasted_iota(jnp.int32, (8, LANES), 1) < tail
    for place in range(QUAT * QUAT // 2):
        left, right = rows_ref[2 * place, :, full:], rows_ref[2 * place + 1, :, full:]
        pair_ref[place] = jnp.where(on_left, left, right)

    def combine(parts, scales):
        total = parts[0] * scales[0]
        for value, scale in zip(parts[1:], scales[1:]):
            total = total + value * scale
        return total

    def square(factors, store, keep_right=False):
        stacked = factors.reshape(QUAT * part, part)
        for tile in range(padded // LANES):
            at = slice(tile * LANES, (tile + 1) * LANES)
            halves = tile * LANES == full
            if halves:
                rows = [pair_ref[place][None] for place in range(QUAT * QUAT // 2)]
            else:
                rows = [rows_ref[place, :, at][None] for place in range(QUAT * QUAT)]
            step = 2 if halves else 1
            groups = QUAT // step
            whole = dot(stacked, repeat[:, at])
            for chunk in range(part // 16):
                spread = [
                    whole[i * part + chunk * 16 : i * part + (chunk + 1) * 16]
                    for i in range(QUAT)
                ]
                spread = [value.reshape(2, 8, LANES) for value in spread]
                for group in range(groups):
                    scales = [rows[i * groups + group] for i in range(QUAT)]
                    total = combine(spread, scales).reshape(16, LANES)
                    values = [total]
                    if halves:
                        values.append(pltpu.roll(total, tail, 1))
                        if keep_right:
                            values.reverse()
                    for place, value in enumerate(values):
                        start = (group * step + place) * part + chunk * 16
                        store(tile, slice(start, start + 16), value.astype(BF16))

    def store_plain(out):
        def store(tile, rows, value):
            width = min(LANES, channels - tile * LANES)
            out[rows, tile * LANES : tile * LANES + width] = value[:, :width]

        return store

    def store_heads(which):
        def store(tile, rows, value):
            if tile * LANES < full:
                at, low, high = which * full + tile * LANES, 0, LANES
            else:
                at, low = 3 * full + which // 2 * LANES, which % 2 * tail
                high = LANES if which == 2 else low + tail
            qkv_out[rows, at + low : at + high] = value[:, low:high]

        return store

    copies[1].wait()
    for tap in range(9):
        square(conv_ref[tap], store_plain(mix_out.at[tap]))
    copies[2].wait()

    @pl.when(lax.axis_index("segment") >= first_skip)
    def _():
        square(skip_ref[...], store_plain(mix_out.at[9]))

    for copy in copies[3:10]:
        copy.wait()
    half = channels // 2
    lane = lax.broadcasted_iota(jnp.int32, (8, channels), 1)
    place = jnp.where(lane < half, lane, lane - half).astype(F32)
    frequency = jnp.exp(-math.log(10000.0) * place / half)
    for batch in range(term_out.shape[0]):
        angles = time_ref[batch].astype(F32) * frequency
        features = jnp.where(lane < half, jnp.cos(angles), jnp.sin(angles)).astype(BF16)
        term_out[batch] = dot(features, proj_ref[...])
    meta_out[0] = flag_ref[0]
    meta_out[1] = offset_ref[0]
    for copy in copies[10:]:
        copy.wait()

    @pl.when(flag_ref[0] == 1)
    def _():
        for which in range(3):
            square(attn_ref[which], store_heads(which), which == 1)
        square(attn_ref[3], store_plain(out_out))

        def widen(value):
            value = value.astype(F32)
            return value[:, :full], jnp.concatenate([value[:, full:]] * 2, axis=1)

        def wide_block(factors, out, rows, fixed, place_of):
            for place in range(QUAT):
                scales = [rule(i, *place_of(fixed, place)) for i in range(QUAT)]
                value = combine([whole for whole, _ in factors], scales)
                out[rows, place * full : (place + 1) * full] = value.astype(BF16)
            for pair in range(QUAT // 2):
                scales = []
                for i in range(QUAT):
                    left = rule(i, *place_of(fixed, 2 * pair))
                    right = rule(i, *place_of(fixed, 2 * pair + 1))
                    scales.append(jnp.where(on_left, left, right)[None])
                halves = [half.reshape(2, 8, LANES) for _, half in factors]
                value = combine(halves, scales).reshape(16, LANES)
                at = QUAT * full + pair * LANES
                out[rows, at : at + LANES] = value.astype(BF16)

        def wide_step(chunk, carry):
            start = pl.multiple_of(chunk * 16, 16)
            ups = [widen(up_ref[i, pl.ds(start, 16), :]) for i in range(QUAT)]
            downs = [widen(down_ref[i, pl.ds(start, 16), :]) for i in range(QUAT)]
            for fixed in range(QUAT):
                rows = pl.ds(pl.multiple_of(fixed * part + start, 16), 16)
                wide_block(ups, up_out, rows, fixed, lambda a, b: (a, b))
                wide_block(downs, down_out, rows, fixed, lambda b, a: (a, b))
            return carry

        lax.fori_loop(0, part // 16, wide_step, 0)


def section_weights(
    first_skip, rule, timesteps, flag, offset, scales, gains, conv, attn, up, down, skip, proj, hidden
):
    channels = proj.shape[0]
    padded = channels // LANES * LANES + LANES
    wide = up.shape[-1]
    operands = (
        rule, timesteps, flag, offset, scales, gains, conv, attn, up, down, skip, proj, hidden,
    )
    return pl.pallas_call(
        functools.partial(weights_kernel, first_skip),
        out_shape=(
            pltpu.VMEM((10, channels, channels), BF16),
            pltpu.VMEM((channels, 8 * LANES), BF16),
            pltpu.VMEM((channels, channels), BF16),
            pltpu.VMEM((channels, QUAT * wide), BF16),
            pltpu.VMEM((channels, QUAT * wide), BF16),
            pltpu.VMEM((hidden.shape[0], 8, channels), F32),
            pltpu.VMEM(gains.shape, F32),
            pltpu.SMEM((2,), jnp.int32),
            pltpu.SMEM(scales.shape, F32),
            pltpu.VMEM(hidden.shape, BF16),
        ),
        in_specs=[HBM] * len(operands),
        out_specs=(VMEM,) * 7 + (SMEM,) * 2 + (VMEM,),
        scratch_shapes=[
            pltpu.SMEM(rule.shape, F32),
            pltpu.SMEM(timesteps.shape, jnp.int32),
            pltpu.SMEM((1,), jnp.int32),
            pltpu.SMEM((1,), jnp.int32),
        ]
        + [pltpu.VMEM(array.shape, BF16) for array in (conv, attn, up, down, skip, proj)]
        + [
            pltpu.VMEM((QUAT * QUAT, 8, padded), F32),
            pltpu.VMEM((QUAT * QUAT // 2, 8, LANES), F32),
            pltpu.SemaphoreType.DMA((len(operands),)),
        ],
        compiler_params=pltpu.CompilerParams(vmem_limit_bytes=12 * MIB),
        name="weights",
    )(*[in_hbm(v) if v.size > 1 else v for v in operands])


def is_active(tick, batches):
    batch = tick - lax.axis_index("segment")
    return (batch >= 0) & (batch < batches)


def shift_columns(normed, columns):
    total = normed.shape[0]
    col = lax.rem(lax.broadcasted_iota(jnp.int32, (total, 1), 0), columns)
    left = jnp.where(col == 0, 0.0, pltpu.roll(normed, 1, 0)).astype(BF16)
    right = jnp.where(col == columns - 1, 0.0, pltpu.roll(normed, total - 1, 0)).astype(BF16)
    return [left, normed.astype(BF16), right]


def inner_kernel(columns, tick, batches, with_skip, *refs):
    if tick is None:
        tick_ref, *refs = refs
        tick = tick_ref[0]
    if with_skip:
        z_ref, *refs = refs
    x_ref, mix_ref, term_ref, gain_ref, sum_ref = refs
    tokens, channels = x_ref.shape

    @pl.when(is_active(tick, batches))
    def _():
        shifted = shift_columns(rms(x_ref[...].astype(F32), gain_ref[0]), columns)
        edge = jnp.zeros((columns, channels), BF16)
        hidden = jnp.broadcast_to(term_ref[0:1, :], (tokens, channels))
        if with_skip:
            hidden = hidden + dot(z_ref[...], mix_ref[9])
        for b in range(3):
            hidden = hidden + dot(shifted[b], mix_ref[3 + b])
        for b in range(3):
            rows = jnp.concatenate([edge, shifted[b][: tokens - columns]], axis=0)
            hidden = hidden + dot(rows, mix_ref[b])
        for b in range(3):
            rows = jnp.concatenate([shifted[b][columns:], edge], axis=0)
            hidden = hidden + dot(rows, mix_ref[6 + b])
        sum_ref[...] = hidden


def attention(normed, qkv_ref, scales_ref, offset, columns):
    tokens = normed.shape[0]
    projected = dot(normed, qkv_ref[...]).astype(BF16)
    tiles = [projected[:, t * LANES : (t + 1) * LANES] for t in range(8)]
    lane = lax.broadcasted_iota(jnp.int32, (tokens, LANES), 1)
    left = lane < HEAD

    groups = lax.broadcasted_iota(jnp.int32, (LANES, LANES), 0) // HEAD
    groups = groups == lax.broadcasted_iota(jnp.int32, (LANES, LANES), 1) // HEAD
    groups = jnp.where(groups, 1.0, 0.0).astype(BF16)
    scaled = [tiles[t].astype(F32) for t in (0, 1, 2, 3, 6)]
    squares = jnp.concatenate([(v * v).astype(BF16) for v in scaled], axis=0)
    inverse = lax.rsqrt(dot(squares, groups) + COS_EPSILON)
    factors = [
        jnp.where(left, scales_ref[0, 0], scales_ref[0, 1]),
        jnp.where(left, scales_ref[0, 2], scales_ref[0, 3]),
        None,
        None,
        jnp.where(left, scales_ref[0, 4], 1.0),
    ]
    units = []
    for place, (value, factor) in enumerate(zip(scaled, factors)):
        norm = inverse[place * tokens : (place + 1) * tokens]
        units.append(value * (norm if factor is None else norm * factor))
    last_key = pltpu.roll(units[4], HEAD, 1).astype(BF16)
    units = [value.astype(BF16) for value in units]

    def window(index):
        return lax.rem(lax.rem(index, columns) - offset + columns, columns) // WIN

    row_window = window(lax.broadcasted_iota(jnp.int32, (tokens, 1), 0))
    same = row_window == window(lax.broadcasted_iota(jnp.int32, (1, tokens), 1))
    zero, one = jnp.zeros((), BF16), jnp.ones((), BF16)

    def weights(query, keys):
        return jnp.where(same, jnp.exp(dot_t(query, keys)), 0.0).astype(BF16)

    mixed = []
    for t in range(2):
        even = weights(jnp.where(left, units[t], zero), units[2 + t])
        odd = weights(jnp.where(left, zero, units[t]), units[2 + t])
        even = dot(even, jnp.where(left, tiles[4 + t], one))
        odd = dot(odd, jnp.where(left, one, tiles[4 + t]))
        sums = pltpu.roll(jnp.where(left, odd, even), HEAD, 1)
        mixed.append((jnp.where(left, even, odd) / sums).astype(BF16))
    even = weights(jnp.where(left, units[4], zero), last_key)
    even = dot(even, jnp.where(left, tiles[7], one))
    mixed.append((even / pltpu.roll(even, HEAD, 1)).astype(BF16)[:, :HEAD])
    return jnp.concatenate(mixed, axis=1)


def outer_kernel(columns, tick, batches, *refs):
    if tick is None:
        tick_ref, *refs = refs
        tick = tick_ref[0]
    (
        meta_ref, scales_ref, x_ref, sum_ref, low_ref, high_ref, prev_ref, mix_ref, qkv_ref,
        proj_ref, up_ref, down_ref, gain_ref, out_ref, first_ref, last_ref,
    ) = refs
    tokens, channels = x_ref.shape
    active = is_active(tick, batches)

    def write(x3):
        value = x3.astype(BF16)
        out_ref[...] = value
        first_ref[...] = value[:columns]
        last_ref[...] = value[tokens - columns :]

    @pl.when(jnp.logical_not(active))
    def _():
        out_ref[...] = prev_ref[...]

    @pl.when(active)
    def _():
        gain = [gain_ref[row] for row in range(3)]
        below = low_ref.shape[0] - columns
        low = shift_columns(rms(low_ref[below:].astype(F32), gain[0]), columns)
        high = shift_columns(rms(high_ref[:columns].astype(F32), gain[0]), columns)
        top = sum_ref[:columns]
        bottom = sum_ref[tokens - columns :]
        for b in range(3):
            top = top + dot(low[b], mix_ref[b])
            bottom = bottom + dot(high[b], mix_ref[6 + b])
        hidden = jnp.concatenate([top, sum_ref[columns : tokens - columns], bottom], axis=0)
        x1 = x_ref[...].astype(F32) + silu(hidden)
        has_block, offset = meta_ref[0], meta_ref[1]

        @pl.when(has_block != 1)
        def _():
            write(x1)

        @pl.when(has_block == 1)
        def _():
            n2 = rms(x1, gain[1]).astype(BF16)
            heads = attention(n2, qkv_ref, scales_ref, offset, columns)
            x2 = x1 + dot(heads, proj_ref[...])
            n3 = rms(x2, gain[2]).astype(BF16)
            act = silu(dot(n3, up_ref[...])).astype(BF16)
            x3 = x2 + dot_t(act, down_ref[...])
            write(x3)


def run_inner(columns, tick, batches, x, z, mix, term, gains):
    static = isinstance(tick, int)
    with_skip = z is not None
    operands = [z] if with_skip else []
    operands += [x, in_vmem(mix), term, in_vmem(gains)]
    specs = [VMEM] * len(operands)
    if not static:
        operands, specs = [tick] + operands, [SMEM] + specs
    return pl.pallas_call(
        functools.partial(inner_kernel, columns, tick if static else None, batches, with_skip),
        out_shape=pltpu.VMEM(x.shape, F32),
        in_specs=specs,
        out_specs=VMEM,
        compiler_params=pltpu.CompilerParams(vmem_limit_bytes=8 * MIB),
        name="inner",
    )(*operands)


def run_outer(columns, tick, batches, x, total, low, high, prev, weights):
    static = isinstance(tick, int)
    mix, qkv, proj, up, down, gains, meta, scales = weights
    operands = [in_smem(meta), in_smem(scales), x, in_vmem(total), low, high, prev]
    operands += [in_vmem(w) for w in (mix, qkv, proj, up, down, gains)]
    specs = [SMEM] * 2 + [VMEM] * (len(operands) - 2)
    if not static:
        operands, specs = [tick] + operands, [SMEM] + specs
    edge = jax.ShapeDtypeStruct((columns, x.shape[1]), BF16)
    return pl.pallas_call(
        functools.partial(outer_kernel, columns, tick if static else None, batches),
        out_shape=(jax.ShapeDtypeStruct(x.shape, BF16), edge, edge),
        in_specs=specs,
        out_specs=(VMEM,) * 3,
        compiler_params=pltpu.CompilerParams(vmem_limit_bytes=8 * MIB),
        name="outer",
    )(*operands)


def shards(
    hidden, timesteps, rule_matrices, conv_factors, time_proj, skip_factors, attn_factors,
    up_factors, down_factors, norm_gains, head_scales, has_block, offsets,
):
    segments = lax.axis_size("segment")
    row_parts = lax.axis_size("rows")
    half = segments // 2
    segment = lax.axis_index("segment")
    batches, height, columns, channels = hidden.shape
    tokens = height * columns
    axes = ("segment", "rows")

    def pairs(sources, step, turn):
        return [
            (s * row_parts + r, (s + step) * row_parts + r + turn)
            for s in sources
            for r in range(row_parts)
            if 0 <= s + step < segments and 0 <= r + turn < row_parts
        ]

    def pass_on(value, sources, step, turn):
        links = pairs(sources, step, turn)
        if not links:
            return jnp.zeros_like(value)
        return lax.ppermute(value, axes, links)

    flat = hidden.reshape(batches, tokens, channels)
    near, far = min(1, segments - 1), min(2, segments - 1)
    low0 = pass_on(flat, [near], -near, 1)
    high0 = pass_on(flat, [far], -far, -1)
    mix, qkv, proj, up, down, terms, gains, meta, scales, flat = section_weights(
        half if batches == 1 else 0,
        rule_matrices[0], timesteps, has_block, offsets, head_scales,
        jnp.transpose(norm_gains, (1, 0, 2)), conv_factors[0], attn_factors[0], up_factors[0],
        jnp.transpose(down_factors[0], (0, 2, 1)), skip_factors[0], time_proj[0], flat,
    )
    weights = (mix, qkv, proj, up, down, gains, meta, scales)

    def section(tick, x, low, high, z, prev, term):
        total = run_inner(columns, tick, batches, x, z, mix, term, gains)
        return run_outer(columns, tick, batches, x, total, low, high, prev, weights)

    def edges_on(out, first, last, sources):
        main = pass_on(out, sources, 1, 0)
        low = pass_on(last, sources, 1, 1)
        high = pass_on(first, sources, 1, -1)
        return main, low, high

    if batches == 1:
        x, low, high = flat[0], low0[0], high0[0]
        out = flat[0]
        skips = []
        for tick in range(segments):
            z = skips[tick - half] if tick >= half else None
            out, first, last = section(tick, x, low, high, z, out, terms[0])
            if tick + 1 < segments:
                x, low, high = edges_on(out, first, last, [tick])
                skips.append(pass_on(out, [tick], half, 0) if tick + half < segments else None)
        return out.reshape(1, batches, height, columns, channels)

    def pick(array, slot):
        return lax.dynamic_index_in_dim(array, slot, 0, keepdims=False)

    def tick_step(tick, state):
        states, received, skip_buffer = state
        slot = jnp.clip(tick - segment, 0, batches - 1)
        own = pick(flat, slot), pick(low0, slot)[tokens - columns :], pick(high0, slot)[:columns]
        x, low, high = [jnp.where(segment == 0, f, r) for f, r in zip(own, received)]
        out, first, last = section(
            jnp.reshape(tick, (1,)), x, low, high, pick(skip_buffer, slot), pick(states, slot),
            pick(terms, slot),
        )
        states = lax.dynamic_update_index_in_dim(states, out, slot, 0)
        passed = edges_on(out, first, last, range(segments))
        arrived = pass_on(out, range(segments), half, 0)
        partner = tick - segment + half
        fits = (segment >= half) & (partner >= 0) & (partner < batches)
        partner_slot = jnp.clip(partner, 0, batches - 1)
        kept = pick(skip_buffer, partner_slot)
        skip_buffer = lax.dynamic_update_index_in_dim(
            skip_buffer, jnp.where(fits, arrived, kept), partner_slot, 0
        )
        return states, passed, skip_buffer

    edge = jnp.zeros((columns, channels), BF16)
    initial = (jnp.zeros_like(flat), (jnp.zeros_like(flat[0]), edge, edge), jnp.zeros_like(flat))
    states = lax.fori_loop(0, batches + segments - 1, tick_step, initial)[0]
    return states.reshape(1, batches, height, columns, channels)


def solution(mesh):
    return jax.shard_map(
        shards,
        mesh=mesh,
        in_specs=(
            P("groups", "rows", None, None),
            P("groups"),
            P("segment", None, None, None),
            P("segment", None, None, None, None),
            P("segment", None, None),
            P("segment", None, None, None),
            P("segment", None, None, None, None),
            P("segment", None, None, None),
            P("segment", None, None, None),
            P("segment", None, None),
            P("segment", None),
            P("segment"),
            P("segment"),
        ),
        out_specs=P("segment", "groups", "rows", None, None),
        check_vma=False,
    )
```
